256 devices in a mesh: sep: 16 (over z, core), tile: 16 (over x, y).
Axes of the slice: x: 4, y: 4, z: 8, core: 2. Of those that a mesh axis runs over, the one named last changes fastest.
Arguments:
- first_frame: float32 [2560, 2560], P('tile'), may hold values from -6 to 6
- second_frames: float32 [16, 2560, 2560], P('sep', 'tile'), may hold values from -6 to 6
- shifts: int32 [2, 16, 80, 80], P(None, 'sep', 'tile'), may hold values from -8 to 8
- fractions: float32 [2, 16, 80, 80], P(None, 'sep', 'tile'), may hold values from 0 to 1
Outputs:
- product_planes: float32 [80, 80, 1024], P('tile', 'sep')
The draws below stay inside these ranges and needn't reach their ends.
All inputs are finite; a program needn't handle non-finite values.
Results may differ from the reference program's by a relative error of at most 0.0003.
Values sent between devices are 32-bit elements; how exact they have to be, the bound alone decides.
No kernel may reach another device: no remote copies, remote signals or barrier semaphores. Data moves between devices by JAX's collectives and lax.ppermute only.
A program may use at most 128 MiB of HBM per device.

```python
import jax
import jax.numpy as jnp
from jax import lax

WIN = 32
MAXSHIFT = 8
HALO = 16
COLS = 2560
SEPS = 16
HEIGHT = 2560
WROWS = 80
WCOLS = 80


def touch_ends(entries, rng, smallest, top_value):
    dims = entries.shape
    place = [jax.random.randint(jax.random.fold_in(rng, axis), (), 0, dims[axis]) for axis in range(len(dims))]
    entries = entries.at[tuple(place)].set(smallest)
    longest = dims.index(max(dims))
    place[longest] = (place[longest] + 1) % dims[longest]
    return entries.at[tuple(place)].set(top_value)


def level_of(rng, extent, cuts, least, largest):
    def one(dim, shards_of):
        heights = jax.random.uniform(jax.random.fold_in(jax.random.fold_in(rng, 6), dim), (shards_of,), jnp.float32, least / len(cuts), largest / len(cuts))
        return jnp.repeat(jnp.exp(heights), extent[dim] // shards_of).reshape((-1,) + (1,) * (len(extent) - dim - 1))

    gain = one(*cuts[0])
    for cut in cuts[1:]:
        gain = gain * one(*cut)
    return gain


def scatter_about(rng, extent, spread, reach, pieces=(), kind=jnp.bfloat16):
    values = spread * jax.random.normal(rng, extent, jnp.float32)
    if pieces:
        values = values * level_of(rng, extent, pieces, -0.22, 0.18)
    return jnp.clip(values, -reach, reach).astype(kind)


def setup_inputs(seed: int = 0) -> dict:
    splits = jax.random.split(jax.random.key(seed), 5)
    first_frame = scatter_about(splits[0], (HEIGHT, COLS), 1.0, 6.0, ((0, 16),), jnp.float32)
    second_frames = scatter_about(splits[1], (SEPS, HEIGHT, COLS), 1.0, 6.0, ((0, 16), (1, 16)), jnp.float32)
    shifts = touch_ends(jax.random.randint(splits[2], (2, SEPS, WROWS, WCOLS), 0 - MAXSHIFT, MAXSHIFT + 1), jax.random.fold_in(splits[2], 1), 0 - MAXSHIFT, MAXSHIFT).astype(jnp.int32)
    fractions = jnp.clip(1.0 * jax.random.uniform(splits[3], (2, SEPS, WROWS, WCOLS), jnp.float32) ** level_of(splits[3], (2, SEPS, WROWS, WCOLS), ((1, 16), (2, 16)), -0.2, 0.2), 0.0, 1.0)
    return dict(first_frame=first_frame, second_frames=second_frames, shifts=shifts, fractions=fractions)


epsilon = 1e-06

def cubic_weights(fraction):
    squared = fraction * fraction
    cubed = squared * fraction
    return jnp.stack([-0.5 * cubed + squared - 0.5 * fraction, 1.5 * cubed - 2.5 * squared + 1.0, -1.5 * cubed + 2.0 * squared + 0.5 * fraction, 0.5 * cubed - 0.5 * squared], axis=-1)

def deform(padded, start_row, start_col, row_taps, col_taps):
    region = lax.dynamic_slice(padded, (start_row, start_col), (WIN + 3, WIN + 3))
    row_mix = row_taps[0] * region[0:WIN] + row_taps[1] * region[1:WIN + 1]
    row_mix = row_mix + row_taps[2] * region[2:WIN + 2] + row_taps[3] * region[3:WIN + 3]
    result = col_taps[0] * row_mix[:, 0:WIN] + col_taps[1] * row_mix[:, 1:WIN + 1]
    return result + col_taps[2] * row_mix[:, 2:WIN + 2] + col_taps[3] * row_mix[:, 3:WIN + 3]

def reference(first_frame, second_frames, shifts, fractions):
    height, frame_cols = first_frame.shape
    win_rows = height // WIN
    win_cols = frame_cols // WIN
    first_win = first_frame.reshape(win_rows, WIN, win_cols, WIN).transpose(0, 2, 1, 3)
    first_win = first_win - lax.optimization_barrier(jnp.mean(first_win, axis=(2, 3), keepdims=True))
    first_pow = lax.optimization_barrier(jnp.mean(first_win * first_win, axis=(2, 3)))
    first_hat = jnp.fft.fft2(first_win)
    row_base = jnp.arange(win_rows, dtype=jnp.int32)[:, None] * WIN + (HALO - 1)
    col_base = jnp.arange(win_cols, dtype=jnp.int32)[None, :] * WIN + (HALO - 1)

    def one_pair(product, inputs):
        second, shift_pair, frac_pair = inputs
        padded = jnp.pad(second, HALO)
        row_start = (row_base + shift_pair[0]).reshape(-1).astype(jnp.int32)
        col_start = (col_base + shift_pair[1]).reshape(-1).astype(jnp.int32)
        row_taps = cubic_weights(frac_pair[0]).reshape(-1, 4)
        col_taps = cubic_weights(frac_pair[1]).reshape(-1, 4)
        second_win = jax.vmap(deform, in_axes=(None, 0, 0, 0, 0))(padded, row_start, col_start, row_taps, col_taps)
        second_win = second_win.reshape(win_rows, win_cols, WIN, WIN)
        second_win = second_win - lax.optimization_barrier(jnp.mean(second_win, axis=(2, 3), keepdims=True))
        second_pow = lax.optimization_barrier(jnp.mean(second_win * second_win, axis=(2, 3)))
        corr = jnp.fft.ifft2(jnp.conj(first_hat) * jnp.fft.fft2(second_win)).real
        scaling = 1.0 / (WIN * WIN * jnp.sqrt((first_pow + epsilon) * (second_pow + epsilon)))
        planes = 1.0 + corr * scaling[:, :, None, None]
        return (product * planes.reshape(win_rows, win_cols, WIN * WIN), None)
    start_prod = jnp.ones((win_rows, win_cols, WIN * WIN), jnp.float32)
    product, unused = lax.scan(one_pair, start_prod, (second_frames, jnp.moveaxis(shifts, 0, 1), jnp.moveaxis(fractions, 0, 1)))
    return product
```

```python
import functools
import math

import jax
import jax.numpy as jnp
import ml_dtypes
import numpy as np
from jax import lax
from jax.experimental import pallas as pl
from jax.experimental.pallas import tpu as pltpu
from jax.sharding import PartitionSpec as P

WIN = 32
HALO = 16
EPS = 1e-06
LANES = 128
BLOCKS = 16
ROOT_HALF = math.sqrt(0.5)


def split_table(table):
    high = table.astype(ml_dtypes.bfloat16)
    low = (table - high.astype(np.float64)).astype(ml_dtypes.bfloat16)
    return high, low


def dft_tables():
    major, minor = np.divmod(np.arange(LANES), WIN)
    forward, backward = [], []
    for unit in (0, 4, 1, 2, 3):
        phase = (np.outer(major, unit + 8 * major) + np.outer(minor, minor)) % WIN
        cos = np.cos(phase * (2.0 * np.pi / WIN))
        sin = np.sin(phase * (2.0 * np.pi / WIN))
        if unit in (0, 4):
            half = np.concatenate([cos, -sin], axis=1)
            forward.append((np.concatenate([half, half]), np.concatenate([half, 0 * half])))
            backward.append(np.concatenate([cos.T, -sin.T]))
        else:
            whole = np.block([[cos, -sin], [sin, cos]])
            forward.append((whole, whole))
            backward.append(2.0 * np.block([[cos.T, sin.T], [-sin.T, cos.T]]))
    fwd_hi = np.stack([split_table(a)[0] for a, _ in forward])
    fwd_lo = np.stack([split_table(b)[1] for _, b in forward])
    ends_hi, ends_lo = split_table(np.stack(backward[:2]))
    mids_hi, mids_lo = split_table(np.stack(backward[2:]))
    return fwd_hi, fwd_lo, ends_hi, ends_lo, mids_hi, mids_lo


def split(value):
    high = value.astype(jnp.bfloat16)
    return high, (value - high.astype(jnp.float32)).astype(jnp.bfloat16)


def dot(left, right):
    return jnp.dot(left, right, preferred_element_type=jnp.float32)


def band_kernel(
    win_rows, slab, tall, shift_ref, taps_ref, first_ref, second_ref, *refs
):
    if tall:
        top_ref, bottom_ref, *refs = refs
    (fwd_hi, fwd_lo, ends_hi, ends_lo, mids_hi, mids_lo, out_ref,
     frame, first, second_win, first_win, pair_ends, pair_hi, pair_lo, powers, back) = refs
    count = len(win_rows)
    block = 5 * count
    windows = BLOCKS * block
    frame_rows = frame.shape[1]
    tiles = second_ref.shape[1] // LANES
    lane = lax.broadcasted_iota(jnp.int32, (8, LANES), 1)
    low_half = lane < 64
    mid_half = (lane >= 32) & (lane < 96)
    even = (lane % 64) < 32

    def rows_of(ref, top, bottom, g):
        cols = slice(g * LANES, (g + 1) * LANES)
        if not tall:
            return ref[16:144, cols]
        return jnp.concatenate([top[:, cols], ref[0:48, cols], ref[112:160, cols], bottom[:, cols]], axis=0)

    wide = lax.broadcasted_iota(jnp.int32, (frame_rows, LANES), 1) < 64
    before = jnp.zeros((frame_rows, LANES), jnp.float32)
    for g in range(tiles):
        here = rows_of(second_ref, top_ref if tall else None, bottom_ref if tall else None, g)
        frame[2 * g + 1] = here
        turned = pltpu.roll(here, 64, 1)
        frame[2 * g] = jnp.where(wide, before, turned)
        before = turned
        for i, row in enumerate(win_rows):
            first[g, WIN * i : WIN * (i + 1), :] = first_ref[
                WIN * row : WIN * (row + 1), g * LANES : (g + 1) * LANES
            ]
    frame[2 * tiles] = jnp.where(wide, before, 0.0)

    def deform(step, carry):
        i, quarter = step // 4, step % 4
        row = win_rows[0] + i * (win_rows[1] - win_rows[0])
        for k in range(20):
            here = row * 80 + quarter * 20 + k
            dest = ((quarter * 4 + k // 5) * block + i * 5 + k % 5) * 8
            start = i * slab + (HALO - 1) + shift_ref[here]
            across = shift_ref[400 + here]
            tile = 2 * (quarter * 5 + k // 4) + (0, 1, 1, 2)[k % 4]
            base = (64, 32, 64, 32)[k % 4]
            lines = [frame[tile, pl.ds(start + m, 8, stride=4), :] for m in range(7)]
            ry = [taps_ref[a * 400 + here] for a in range(4)]
            rx = [taps_ref[(4 + a) * 400 + here] for a in range(4)]
            placed = []
            for j in range(4):
                mixed = (ry[0] * lines[j] + ry[1] * lines[j + 1]) + (ry[2] * lines[j + 2] + ry[3] * lines[j + 3])
                placed.append(pltpu.roll(mixed, (32 * j - base + 1 + 256 - across) & 127, 1))
            one = jnp.where(low_half, placed[0], placed[2])
            two = jnp.where(mid_half, placed[1], placed[3])
            total = rx[0] * jnp.where(even, one, two)
            for b in range(1, 4):
                total = total + rx[b] * jnp.where(even, pltpu.roll(one, LANES - b, 1), pltpu.roll(two, LANES - b, 1))
            second_win[pl.ds(pl.multiple_of(dest, 8), 8), :] = total
        for g in range(5):
            lines = [first[quarter * 5 + g, pl.ds(i * WIN + j, 8, stride=4), :] for j in range(4)]
            for w in range(4):
                k = 4 * g + w
                dest = ((quarter * 4 + k // 5) * block + i * 5 + k % 5) * 8
                turned = [pltpu.roll(lines[j], (32 * (j - w)) % LANES, 1) if j != w else lines[j] for j in range(4)]
                pair = jnp.where(even, turned[0], turned[1])
                other = jnp.where(even, turned[2], turned[3])
                first_win[pl.ds(pl.multiple_of(dest, 8), 8), :] = jnp.where(low_half, pair, other)
        return carry

    lax.fori_loop(0, 4 * count, deform, 0)

    def lift(step, carry):
        w = pl.multiple_of(step * 16, 16)
        power = []
        for side, source in enumerate((first_win, second_win)):
            at = pl.ds(pl.multiple_of(side * windows + step * 16, 16), 16)
            x = [source[pl.ds(step * 128 + l, 16, stride=8), :] for l in range(8)]
            total = ((x[0] + x[1]) + (x[2] + x[3])) + ((x[4] + x[5]) + (x[6] + x[7]))
            mean = jnp.sum(total, axis=1, keepdims=True) * (1.0 / 1024.0)
            x = [v - mean for v in x]
            q = [v * v for v in x]
            total = ((q[0] + q[1]) + (q[2] + q[3])) + ((q[4] + q[5]) + (q[6] + q[7]))
            power.append(jnp.sum(total, axis=1, keepdims=True) * (1.0 / 1024.0) + EPS)
            s = [x[l] + x[l + 4] for l in range(4)]
            d = [x[l] - x[l + 4] for l in range(4)]
            e, o = s[0] + s[2], s[1] + s[3]
            p, m = (d[1] + d[3]) * ROOT_HALF, (d[1] - d[3]) * ROOT_HALF
            for unit, value in enumerate((e + o, e - o)):
                high, low = split(value)
                pair_ends[unit, at, 0:LANES] = high
                pair_ends[unit, at, LANES : 2 * LANES] = low
            mids = ((d[0] + m, -(d[2] + p)), (s[0] - s[2], s[3] - s[1]), (d[0] - m, d[2] - p))
            for unit, parts in enumerate(mids):
                for half, value in enumerate(parts):
                    high, low = split(value)
                    pair_hi[unit, at, half * LANES : (half + 1) * LANES] = high
                    pair_lo[unit, at, half * LANES : (half + 1) * LANES] = low
        scale = (1.0 / (1024.0 * 1024.0)) / jnp.sqrt(power[0] * power[1])
        powers[pl.ds(w, 16), :] = jnp.broadcast_to(scale, (16, LANES))
        return carry

    lax.fori_loop(0, windows // 16, lift, 0)

    for unit in range(5):
        if unit < 2:
            spectrum = dot(pair_ends[unit], fwd_hi[unit]) + dot(
                pair_ends[unit, :, 0:LANES], fwd_lo[unit, 0:LANES]
            )
        else:
            spectrum = (
                dot(pair_hi[unit - 2], fwd_hi[unit])
                + dot(pair_lo[unit - 2], fwd_hi[unit])
                + dot(pair_hi[unit - 2], fwd_lo[unit])
            )
        fr, fi = spectrum[:windows, :LANES], spectrum[:windows, LANES:]
        sr, si = spectrum[windows:, :LANES], spectrum[windows:, LANES:]
        re_hi, re_lo = split(fr * sr + fi * si)
        im_hi, im_lo = split(fr * si - fi * sr)
        high = jnp.concatenate([re_hi, im_hi], axis=1)
        low = jnp.concatenate([re_lo, im_lo], axis=1)
        if unit < 2:
            table_hi, table_lo = ends_hi[unit], ends_lo[unit]
        else:
            table_hi, table_lo = mids_hi[unit - 2], mids_lo[unit - 2]
        result = dot(high, table_hi) + dot(low, table_hi) + dot(high, table_lo)
        if unit < 2:
            back[unit] = result
        else:
            back[2 * unit - 2] = result[:, :LANES]
            back[2 * unit - 1] = result[:, LANES:]

    def lower(step, carry):
        at = pl.ds(pl.multiple_of(step * 16, 16), 16)
        b0, b4, b1r, b1i, b2r, b2i, b3r, b3i = (back[u, at, :] for u in range(8))
        scale = powers[at, :]
        plus, minus = b0 + b4, b0 - b4
        evens = (plus + b2r, minus - b2i, plus - b2r, minus + b2i)
        u, v = (b1r - b3r) * ROOT_HALF, (b1i + b3i) * ROOT_HALF
        odds = (b1r + b3r, u - v, b3i - b1i, -(u + v))
        for l in range(4):
            out_ref[pl.ds(step * 128 + l, 16, stride=8), :] = 1.0 + (evens[l] + odds[l]) * scale
            out_ref[pl.ds(step * 128 + l + 4, 16, stride=8), :] = 1.0 + (evens[l] - odds[l]) * scale
        return carry

    lax.fori_loop(0, windows // 16, lower, 0)


def band_planes(win_rows, shifts, taps, first, second, halos, tables, interpret=False):
    count = len(win_rows)
    windows = BLOCKS * 5 * count
    tiles = second.shape[1] // LANES
    tall = halos is not None
    arrays = [first, second, *(halos or ()), *tables]
    vmem = pl.BlockSpec(memory_space=pltpu.VMEM)
    smem = pl.BlockSpec(memory_space=pltpu.SMEM)
    f32, bf16 = jnp.float32, jnp.bfloat16
    out = pl.pallas_call(
        functools.partial(band_kernel, win_rows, 64 if tall else 32, tall),
        out_shape=jax.ShapeDtypeStruct((windows * 8, LANES), f32),
        in_specs=[smem, smem] + [vmem] * len(arrays),
        out_specs=vmem,
        scratch_shapes=[
            pltpu.VMEM((2 * tiles + 1, 128, LANES), f32),
            pltpu.VMEM((tiles, WIN * count, LANES), f32),
            pltpu.VMEM((windows * 8, LANES), f32),
            pltpu.VMEM((windows * 8, LANES), f32),
            pltpu.VMEM((2, 2 * windows, 2 * LANES), bf16),
            pltpu.VMEM((3, 2 * windows, 2 * LANES), bf16),
            pltpu.VMEM((3, 2 * windows, 2 * LANES), bf16),
            pltpu.VMEM((windows, LANES), f32),
            pltpu.VMEM((8, windows, LANES), f32),
        ],
        compiler_params=pltpu.CompilerParams(vmem_limit_bytes=40 * 1024 * 1024),
        interpret=interpret,
        name="band_tall" if tall else "band",
    )(shifts, taps, *arrays)
    return out


def cubic_weights(fraction):
    squared = fraction * fraction
    cubed = squared * fraction
    return (
        -0.5 * cubed + squared - 0.5 * fraction,
        1.5 * cubed - 2.5 * squared + 1.0,
        -1.5 * cubed + 2.0 * squared + 0.5 * fraction,
        0.5 * cubed - 0.5 * squared,
    )


def local(first, seconds, shifts, fractions):
    second = seconds[0]
    top = lax.ppermute(second[-HALO:], "tile", [(i, i + 1) for i in range(15)])
    bottom = lax.ppermute(second[:HALO], "tile", [(i + 1, i) for i in range(15)])
    taps = jnp.stack([*cubic_weights(fractions[0]), *cubic_weights(fractions[1])]).reshape(-1)
    shifts = shifts.reshape(-1)
    tables = [jnp.asarray(t) for t in dft_tables()]
    inner = band_planes((1, 2, 3), shifts, taps, first, second, None, tables).reshape(BLOCKS, 15, 1024)
    outer = band_planes((0, 4), shifts, taps, first, second, (top, bottom), tables).reshape(BLOCKS, 10, 1024)
    both = jnp.concatenate([outer[:, :5], inner, outer[:, 5:]], axis=1)
    everything = lax.all_to_all(both, "sep", 0, 0)
    return jnp.prod(everything, axis=0).reshape(5, 5, 1024)


def solution(mesh):
    in_specs = (
        P("tile", None),
        P("sep", "tile", None),
        P(None, "sep", "tile", None),
        P(None, "sep", "tile", None),
    )
    out_specs = P("tile", "sep", None)
    return jax.shard_map(local, mesh=mesh, in_specs=in_specs, out_specs=out_specs, check_vma=False)
```

```python
import functools
import math

import jax
import jax.numpy as jnp
import ml_dtypes
import numpy as np
from jax import lax
from jax.experimental import pallas as pl
from jax.experimental.pallas import tpu as pltpu
from jax.sharding import PartitionSpec as P

WIN = 32
HALO = 16
EPS = 1e-06
LANES = 128
BLOCKS = 16
ROOT_HALF = math.sqrt(0.5)


def split_table(table):
    high = table.astype(ml_dtypes.bfloat16)
    low = (table - high.astype(np.float64)).astype(ml_dtypes.bfloat16)
    return high, low


def dft_tables():
    major, minor = np.divmod(np.arange(LANES), WIN)
    forward, backward = [], []
    for unit in (0, 4, 1, 2, 3):
        phase = (np.outer(major, unit + 8 * major) + np.outer(minor, minor)) % WIN
        cos = np.cos(phase * (2.0 * np.pi / WIN))
        sin = np.sin(phase * (2.0 * np.pi / WIN))
        if unit in (0, 4):
            half = np.concatenate([cos, -sin], axis=1)
            forward.append((np.concatenate([half, half]), np.concatenate([half, 0 * half])))
            backward.append(np.concatenate([cos.T, -sin.T]))
        else:
            whole = np.block([[cos, -sin], [sin, cos]])
            forward.append((whole, whole))
            backward.append(2.0 * np.block([[cos.T, sin.T], [-sin.T, cos.T]]))
    fwd_hi = np.stack([split_table(a)[0] for a, _ in forward])
    fwd_lo = np.stack([split_table(b)[1] for _, b in forward])
    ends_hi, ends_lo = split_table(np.stack(backward[:2]))
    mids_hi, mids_lo = split_table(np.stack(backward[2:]))
    return fwd_hi, fwd_lo, ends_hi, ends_lo, mids_hi, mids_lo


def split(value):
    high = value.astype(jnp.bfloat16)
    return high, (value - high.astype(jnp.float32)).astype(jnp.bfloat16)


def dot(left, right):
    return jnp.dot(left, right, preferred_element_type=jnp.float32)


def cubic_weights(fraction):
    squared = fraction * fraction
    cubed = squared * fraction
    return (
        -0.5 * cubed + squared - 0.5 * fraction,
        1.5 * cubed - 2.5 * squared + 1.0,
        -1.5 * cubed + 2.0 * squared + 0.5 * fraction,
        0.5 * cubed - 0.5 * squared,
    )


def band_kernel(win_rows, slab, tall, shift_ref, fraction_ref, first_hbm, second_hbm, *refs):
    halos, refs = (refs[:2], refs[2:]) if tall else ((), refs)
    tables_hbm, refs = refs[:6], refs[6:]
    (keep_ref, away_ref, frame, first, shifted, second_win, first_win, pair_ends, pair_hi, pair_lo, powers,
     back, taps_vmem, taps_ref, *tables, frame_sems, first_sems, table_sems) = refs
    fwd_hi, fwd_lo, ends_hi, ends_lo, mids_hi, mids_lo = tables
    count = len(win_rows)
    block = 5 * count
    windows = BLOCKS * block
    frame_rows = frame.shape[1]
    tiles = second_hbm.shape[1] // LANES
    lane = lax.broadcasted_iota(jnp.int32, (8, LANES), 1)
    low_half = lane < 64
    mid_half = (lane >= 32) & (lane < 96)
    even = (lane % 64) < 32
    own = lax.axis_index("sep")
    own_chip, own_core = own >> 1, own & 1

    if tall:
        pieces = ((halos[0], 0, 0, 16), (second_hbm, 0, 16, 48), (second_hbm, 112, 64, 48), (halos[1], 0, 112, 16))
    else:
        pieces = ((second_hbm, 16, 0, 128),)

    def frame_copies(g):
        return [
            pltpu.make_async_copy(
                ref.at[pl.ds(source, rows), pl.ds(g * LANES, LANES)],
                frame.at[2 * g + 1, pl.ds(target, rows), :],
                frame_sems.at[n, g],
            )
            for n, (ref, source, target, rows) in enumerate(pieces)
        ]

    if tall:
        lines = tuple((WIN * row, WIN * i, WIN) for i, row in enumerate(win_rows))
    else:
        lines = ((WIN * win_rows[0], 0, WIN * count),)

    def first_copies(g):
        return [
            pltpu.make_async_copy(
                first_hbm.at[pl.ds(source, rows), pl.ds(g * LANES, LANES)],
                first.at[g, pl.ds(target, rows), :],
                first_sems.at[n, g],
            )
            for n, (source, target, rows) in enumerate(lines)
        ]

    table_copies = [
        pltpu.make_async_copy(source, target, table_sems.at[n])
        for n, (source, target) in enumerate(zip(tables_hbm, tables, strict=True))
    ]
    for copies in (frame_copies, first_copies):
        for g in range(tiles):
            for copy in copies(g):
                copy.start()
    for copy in table_copies:
        copy.start()

    for axis in range(2):
        for a, values in enumerate(cubic_weights(fraction_ref[axis, 0])):
            taps_vmem[2 * a + axis, 0:5, 0:80] = values
    taps_copy = pltpu.make_async_copy(taps_vmem, taps_ref, table_sems.at[6])
    taps_copy.start()

    wide = lax.broadcasted_iota(jnp.int32, (frame_rows, LANES), 1) < 64
    before = jnp.zeros((frame_rows, LANES), jnp.float32)
    for g in range(tiles):
        for copy in frame_copies(g):
            copy.wait()
        turned = pltpu.roll(frame[2 * g + 1], 64, 1)
        frame[2 * g] = jnp.where(wide, before, turned)
        before = turned
    frame[2 * tiles] = jnp.where(wide, before, 0.0)

    for g in range(tiles):
        for copy in first_copies(g):
            copy.wait()

    def place(chip, core, i):
        turn = chip - own_chip if core == 0 else own_chip - chip
        return ((((own_core ^ core) * 8 + ((3 * turn) & 7)) * block) + i * 5) * 8

    def gather(step, carry):
        i, quarter = step >> 2, step & 3
        base = [place(quarter * 2 + (n >> 1), n & 1, i) for n in range(4)]
        for g in range(5):
            parts = [first[quarter * 5 + g, pl.ds(i * WIN + j, 8, stride=4), :] for j in range(4)]
            for w in range(4):
                k = 4 * g + w
                turned = [pltpu.roll(parts[j], (32 * (j - w)) % LANES, 1) if j != w else parts[j] for j in range(4)]
                pair = jnp.where(even, turned[0], turned[1])
                other = jnp.where(even, turned[2], turned[3])
                dest = pl.multiple_of(base[k // 5] + (k % 5) * 8, 8)
                first_win[pl.ds(dest, 8), :] = jnp.where(low_half, pair, other)
        return carry

    lax.fori_loop(0, 4 * count, gather, 0)

    taps_copy.wait()

    def mix_rows(step, k):
        i, chip = step >> 3, step & 7
        row, column = win_rows[0] + i * (win_rows[1] - win_rows[0]), chip * 10 + k
        start = i * slab + (HALO - 1) + shift_ref[0, 0, row, column]
        across = shift_ref[1, 0, row, column]
        tile = chip * 5 + (k + 1) // 2
        rows = [frame[tile, pl.ds(start + m, 8, stride=4), :] for m in range(7)]
        ry = [taps_ref[2 * a, row, column] for a in range(4)]
        turned = []
        for j in range(4):
            mixed = (ry[0] * rows[j] + ry[1] * rows[j + 1]) + (ry[2] * rows[j + 2] + ry[3] * rows[j + 3])
            turned.append(pltpu.roll(mixed, (32 * j - (64, 32)[k % 2] + 1 + 256 - across) & 127, 1))
        shifted[k, 0] = jnp.where(low_half, turned[0], turned[2])
        shifted[k, 1] = jnp.where(mid_half, turned[1], turned[3])

    def mix_columns(step, k, base):
        i, chip = step >> 3, step & 7
        row, column = win_rows[0] + i * (win_rows[1] - win_rows[0]), chip * 10 + k
        rx = [taps_ref[2 * a + 1, row, column] for a in range(4)]
        one, two = shifted[k, 0], shifted[k, 1]
        total = rx[0] * jnp.where(even, one, two)
        for b in range(1, 4):
            total = total + rx[b] * jnp.where(even, pltpu.roll(one, LANES - b, 1), pltpu.roll(two, LANES - b, 1))
        second_win[pl.ds(pl.multiple_of(base[k // 5] + (k % 5) * 8, 8), 8), :] = total

    steps = 8 * count
    for k in range(10):
        mix_rows(0, k)

    def deform(step, carry):
        base = [place(step & 7, core, step >> 3) for core in range(2)]
        later = jnp.minimum(step + 1, steps - 1)
        for k in range(10):
            mix_columns(step, k, base)
            mix_rows(later, k)
        return carry

    lax.fori_loop(0, steps, deform, 0)

    def lift(step, carry):
        w = pl.multiple_of(step * 16, 16)
        power = []
        for side, source in enumerate((first_win, second_win)):
            at = pl.ds(pl.multiple_of(side * windows + step * 16, 16), 16)
            x = [source[pl.ds(step * 128 + l, 16, stride=8), :] for l in range(8)]
            total = ((x[0] + x[1]) + (x[2] + x[3])) + ((x[4] + x[5]) + (x[6] + x[7]))
            mean = jnp.sum(total, axis=1, keepdims=True) * (1.0 / 1024.0)
            x = [v - mean for v in x]
            q = [v * v for v in x]
            total = ((q[0] + q[1]) + (q[2] + q[3])) + ((q[4] + q[5]) + (q[6] + q[7]))
            power.append(jnp.sum(total, axis=1, keepdims=True) * (1.0 / 1024.0) + EPS)
            s = [x[l] + x[l + 4] for l in range(4)]
            d = [x[l] - x[l + 4] for l in range(4)]
            e, o = s[0] + s[2], s[1] + s[3]
            p, m = (d[1] + d[3]) * ROOT_HALF, (d[1] - d[3]) * ROOT_HALF
            for unit, value in enumerate((e + o, e - o)):
                high, low = split(value)
                pair_ends[unit, at, 0:LANES] = high
                pair_ends[unit, at, LANES : 2 * LANES] = low
            mids = ((d[0] + m, -(d[2] + p)), (s[0] - s[2], s[3] - s[1]), (d[0] - m, d[2] - p))
            for unit, parts in enumerate(mids):
                for half, value in enumerate(parts):
                    high, low = split(value)
                    pair_hi[unit, at, half * LANES : (half + 1) * LANES] = high
                    pair_lo[unit, at, half * LANES : (half + 1) * LANES] = low
        scale = (1.0 / (1024.0 * 1024.0)) / jnp.sqrt(power[0] * power[1])
        powers[pl.ds(w, 16), :] = jnp.broadcast_to(scale, (16, LANES))
        return carry

    lax.fori_loop(0, windows // 16, lift, 0, unroll=5)
    for copy in table_copies:
        copy.wait()

    for unit in range(5):
        if unit < 2:
            spectrum = dot(pair_ends[unit], fwd_hi[unit]) + dot(
                pair_ends[unit, :, 0:LANES], fwd_lo[unit, 0:LANES]
            )
        else:
            spectrum = (
                dot(pair_hi[unit - 2], fwd_hi[unit])
                + dot(pair_lo[unit - 2], fwd_hi[unit])
                + dot(pair_hi[unit - 2], fwd_lo[unit])
            )
        fr, fi = spectrum[:windows, :LANES], spectrum[:windows, LANES:]
        sr, si = spectrum[windows:, :LANES], spectrum[windows:, LANES:]
        re_hi, re_lo = split(fr * sr + fi * si)
        im_hi, im_lo = split(fr * si - fi * sr)
        high = jnp.concatenate([re_hi, im_hi], axis=1)
        low = jnp.concatenate([re_lo, im_lo], axis=1)
        if unit < 2:
            table_hi, table_lo = ends_hi[unit], ends_lo[unit]
        else:
            table_hi, table_lo = mids_hi[unit - 2], mids_lo[unit - 2]
        result = dot(high, table_hi) + dot(low, table_hi) + dot(high, table_lo)
        if unit < 2:
            back[unit] = result
        else:
            back[2 * unit - 2] = result[:, :LANES]
            back[2 * unit - 1] = result[:, LANES:]

    for part, out_ref in enumerate((away_ref, keep_ref)):

        def lower(step, carry, out_ref=out_ref, offset=(1 - part) * (windows // 2)):
            at = pl.ds(pl.multiple_of(offset + step * 8, 8), 8)
            b0, b4, b1r, b1i, b2r, b2i, b3r, b3i = (back[u, at, :] for u in range(8))
            scale = powers[at, :]
            plus, minus = b0 + b4, b0 - b4
            evens = (plus + b2r, minus - b2i, plus - b2r, minus + b2i)
            u, v = (b1r - b3r) * ROOT_HALF, (b1i + b3i) * ROOT_HALF
            odds = (b1r + b3r, u - v, b3i - b1i, -(u + v))
            for l in range(4):
                out_ref[pl.ds(step * 64 + l, 8, stride=8), :] = 1.0 + (evens[l] + odds[l]) * scale
                out_ref[pl.ds(step * 64 + l + 4, 8, stride=8), :] = 1.0 + (evens[l] - odds[l]) * scale
            return carry

        lax.fori_loop(0, windows // 16, lower, 0, unroll=5)


def band_planes(win_rows, shifts, fractions, first, second, halos, tables, interpret=False):
    count = len(win_rows)
    windows = BLOCKS * 5 * count
    tiles = second.shape[1] // LANES
    tall = halos is not None
    arrays = [first, second, *(halos or ()), *tables]
    vmem = pl.BlockSpec(memory_space=pltpu.VMEM)
    smem = pl.BlockSpec(memory_space=pltpu.SMEM)
    hbm = pl.BlockSpec(memory_space=pltpu.HBM)
    f32, bf16 = jnp.float32, jnp.bfloat16
    half = jax.ShapeDtypeStruct((windows * 4, LANES), f32)
    return pl.pallas_call(
        functools.partial(band_kernel, win_rows, 64 if tall else 32, tall),
        out_shape=[half, half],
        in_specs=[smem, vmem] + [hbm] * len(arrays),
        out_specs=[vmem, vmem],
        scratch_shapes=[
            pltpu.VMEM((2 * tiles + 1, 128, LANES), f32),
            pltpu.VMEM((tiles, WIN * count, LANES), f32),
            pltpu.VMEM((10, 2, 8, LANES), f32),
            pltpu.VMEM((windows * 8, LANES), f32),
            pltpu.VMEM((windows * 8, LANES), f32),
            pltpu.VMEM((2, 2 * windows, 2 * LANES), bf16),
            pltpu.VMEM((3, 2 * windows, 2 * LANES), bf16),
            pltpu.VMEM((3, 2 * windows, 2 * LANES), bf16),
            pltpu.VMEM((windows, LANES), f32),
            pltpu.VMEM((8, windows, LANES), f32),
            pltpu.VMEM((8, 8, LANES), f32),
            pltpu.SMEM((8, 8, LANES), f32),
            *(pltpu.VMEM(t.shape, t.dtype) for t in tables),
            pltpu.SemaphoreType.DMA((4, tiles)),
            pltpu.SemaphoreType.DMA((2, tiles)),
            pltpu.SemaphoreType.DMA((7,)),
        ],
        compiler_params=pltpu.CompilerParams(vmem_limit_bytes=24 * 1024 * 1024),
        interpret=interpret,
        name="band_tall" if tall else "band",
    )(shifts, fractions, *(pltpu.with_memory_space_constraint(a, pltpu.HBM) for a in arrays))


def along_z(array, hops):
    pairs = [(2 * z + c, 2 * ((z + (hops, -hops)[c]) % 8) + c) for z in range(8) for c in range(2)]
    return lax.ppermute(array, "sep", pairs)


def reduced(keep, away):
    size = keep.shape[0] // 8
    parts = keep * lax.ppermute(away, "sep", [(s, s ^ 1) for s in range(16)])
    ahead = along_z(parts[3 * size : 5 * size], 1)
    behind = along_z(parts[5 * size :], -1)
    near = parts[: 3 * size] * behind
    third = along_z(near[size : 2 * size] * ahead[size:], 3)
    sixth = along_z(near[2 * size :], -2)
    return near[:size] * ahead[:size] * third * sixth


def local(first, seconds, shifts, fractions):
    second = seconds[0]
    top = lax.ppermute(second[-HALO:], "tile", [(i, i + 1) for i in range(15)])
    bottom = lax.ppermute(second[:HALO], "tile", [(i + 1, i) for i in range(15)])
    tables = [jnp.asarray(t) for t in dft_tables()]
    inner = band_planes((1, 2, 3), shifts, fractions, first, second, None, tables)
    inner, (top, bottom) = lax.optimization_barrier((inner, (top, bottom)))
    outer = band_planes((0, 4), shifts, fractions, first, second, (top, bottom), tables)
    inner = reduced(*inner).reshape(3, 5, 1024)
    outer = reduced(*outer).reshape(2, 5, 1024)
    return jnp.concatenate([outer[:1], inner, outer[1:]], axis=0)


def solution(mesh):
    in_specs = (
        P("tile", None),
        P("sep", "tile", None),
        P(None, "sep", "tile", None),
        P(None, "sep", "tile", None),
    )
    out_specs = P("tile", "sep", None)
    return jax.shard_map(local, mesh=mesh, in_specs=in_specs, out_specs=out_specs, check_vma=False)
```

```python
import functools
import math

import jax
import jax.numpy as jnp
import ml_dtypes
import numpy as np
from jax import lax
from jax.experimental import pallas as pl
from jax.experimental.pallas import tpu as pltpu
from jax.sharding import PartitionSpec as P

WIN = 32
HALO = 16
EPS = 1e-06
LANES = 128
BLOCKS = 16
ROOT_HALF = math.sqrt(0.5)


def split_table(table):
    high = table.astype(ml_dtypes.bfloat16)
    low = (table - high.astype(np.float64)).astype(ml_dtypes.bfloat16)
    return high, low


def dft_tables():
    major, minor = np.divmod(np.arange(LANES), WIN)
    high, low = [], []
    for unit in (0, 4, 1, 2, 3):
        phase = (np.outer(major, unit + 8 * major) + np.outer(minor, minor)) % WIN
        cos = np.cos(phase * (2.0 * np.pi / WIN))
        sin = np.sin(phase * (2.0 * np.pi / WIN))
        if unit in (0, 4):
            table = np.concatenate([np.concatenate([cos, -sin], axis=1)] * 2)
        else:
            table = np.block([[cos, -sin], [sin, cos]])
        high.append(split_table(table)[0])
        low.append(split_table(table)[1])
    return np.stack(high), np.stack(low)


def split(value):
    high = value.astype(jnp.bfloat16)
    return high, (value - high.astype(jnp.float32)).astype(jnp.bfloat16)


def dot(left, right):
    return jnp.dot(left, right, preferred_element_type=jnp.float32)


def dot_back(left, right):
    return lax.dot_general(left, right, (((1,), (1,)), ((), ())), preferred_element_type=jnp.float32)


def cubic_weights(fraction):
    squared = fraction * fraction
    cubed = squared * fraction
    return (
        -0.5 * cubed + squared - 0.5 * fraction,
        1.5 * cubed - 2.5 * squared + 1.0,
        -1.5 * cubed + 2.0 * squared + 0.5 * fraction,
        0.5 * cubed - 0.5 * squared,
    )


def masks():
    lane = lax.broadcasted_iota(jnp.int32, (8, LANES), 1)
    return lane, lane < 64, (lane % 64) < 32


def place(chip, core, i, block):
    own = lax.axis_index("sep")
    own_chip, own_core = own >> 1, own & 1
    turn = chip - own_chip if core == 0 else own_chip - chip
    return ((((own_core ^ core) * 8 + ((3 * turn) & 7)) * block) + i * 5) * 8


def lift_windows(source, pair_ends, pair_hi, pair_lo, finish):
    def lift(step, carry):
        at = pl.ds(pl.multiple_of(step * 16, 16), 16)
        x = [source[pl.ds(step * 128 + l, 16, stride=8), :] for l in range(8)]
        total = ((x[0] + x[1]) + (x[2] + x[3])) + ((x[4] + x[5]) + (x[6] + x[7]))
        mean = jnp.sum(total, axis=1, keepdims=True) * (1.0 / 1024.0)
        x = [v - mean for v in x]
        q = [v * v for v in x]
        total = ((q[0] + q[1]) + (q[2] + q[3])) + ((q[4] + q[5]) + (q[6] + q[7]))
        finish(at, jnp.sum(total, axis=1, keepdims=True) * (1.0 / 1024.0) + EPS)
        s = [x[l] + x[l + 4] for l in range(4)]
        d = [x[l] - x[l + 4] for l in range(4)]
        e, o = s[0] + s[2], s[1] + s[3]
        p, m = (d[1] + d[3]) * ROOT_HALF, (d[1] - d[3]) * ROOT_HALF
        for unit, value in enumerate((e + o, e - o)):
            high, low = split(value)
            pair_ends[unit, at, 0:LANES] = high
            pair_ends[unit, at, LANES : 2 * LANES] = low
        mids = ((d[0] + m, -(d[2] + p)), (s[0] - s[2], s[3] - s[1]), (d[0] - m, d[2] - p))
        for unit, parts in enumerate(mids):
            for half, value in enumerate(parts):
                high, low = split(value)
                pair_hi[unit, at, half * LANES : (half + 1) * LANES] = high
                pair_lo[unit, at, half * LANES : (half + 1) * LANES] = low
        return carry

    lax.fori_loop(0, source.shape[0] // 128, lift, 0, unroll=5)


def spectrum_of(unit, pair_ends, pair_hi, pair_lo, table_hi, table_lo):
    hi, lo = table_hi[unit], table_lo[unit]
    if unit < 2:
        return dot(pair_ends[unit], hi) + dot(pair_ends[unit, :, 0:LANES], lo[0:LANES])
    return dot(pair_hi[unit - 2], hi) + dot(pair_lo[unit - 2], hi) + dot(pair_hi[unit - 2], lo)


def first_kernel(first_hbm, high_hbm, low_hbm, spectra_ref, power_ref,
                 first, first_win, pair_ends, pair_hi, pair_lo, table_hi, table_lo, first_sems, table_sems):
    win_rows = first_hbm.shape[0] // WIN
    block = first_win.shape[0] // 8 // BLOCKS
    lane, low_half, even = masks()
    outer_blocks = (lane < 32) | (lane >= 96)
    first_copies = [
        pltpu.make_async_copy(first_hbm.at[:, pl.ds(g * LANES, LANES)], first.at[g], first_sems.at[g])
        for g in range(first.shape[0])
    ]
    table_copies = [
        pltpu.make_async_copy(high_hbm, table_hi, table_sems.at[0]),
        pltpu.make_async_copy(low_hbm, table_lo, table_sems.at[1]),
    ]
    for copy in first_copies + table_copies:
        copy.start()
    for copy in first_copies:
        copy.wait()

    def gather(step, carry):
        i, quarter = step >> 2, step & 3
        base = [place(quarter * 2 + (n >> 1), n & 1, i, block) for n in range(4)]
        for g in range(5):
            v = [first[quarter * 5 + g, pl.ds(i * WIN + j, 8, stride=4), :] for j in range(4)]
            turned = pltpu.roll(jnp.where(outer_blocks, v[2], v[0]), 64, 1)
            p = jnp.where(low_half, jnp.where(even, v[0], v[2]), turned)
            q = jnp.where(low_half, turned, jnp.where(even, v[2], v[0]))
            turned = pltpu.roll(jnp.where(low_half, v[3], v[1]), 64, 1)
            r = jnp.where(low_half, v[1], turned)
            s = jnp.where(low_half, turned, v[3])
            for w, (one, two) in ((0, (p, r)), (2, (q, s))):
                turned = pltpu.roll(jnp.where(even, two, one), 32, 1)
                for k, value in (
                    (4 * g + w, jnp.where(even, one, turned)),
                    (4 * g + w + 1, jnp.where(even, turned, two)),
                ):
                    first_win[pl.ds(pl.multiple_of(base[k // 5] + (k % 5) * 8, 8), 8), :] = value
        return carry

    lax.fori_loop(0, 4 * win_rows, gather, 0, unroll=2)


    def finish(at, power):
        power_ref[at, :] = jnp.broadcast_to(power, (16, LANES))

    lift_windows(first_win, pair_ends, pair_hi, pair_lo, finish)
    for copy in table_copies:
        copy.wait()
    for unit in range(5):
        spectra_ref[unit] = spectrum_of(unit, pair_ends, pair_hi, pair_lo, table_hi, table_lo)


def band_kernel(shift_hbm, fraction_hbm, second_hbm, top_hbm, bottom_hbm, high_hbm, low_hbm, spectra_ref, power_ref,
                keep_ref, away_ref, frame, swapped, shifted, second_win,
                pair_ends, pair_hi, pair_lo, powers, back, fraction_ref, shift_ref, taps_vmem, taps_ref,
                table_hi, table_lo, frame_sems, small_sems):
    windows = second_win.shape[0] // 8
    band = second_hbm.shape[0]
    win_rows = band // WIN
    block = windows // BLOCKS
    tiles = second_hbm.shape[1] // LANES
    lane, low_half, even = masks()

    small_copies = [
        pltpu.make_async_copy(fraction_hbm, fraction_ref, small_sems.at[0]),
        pltpu.make_async_copy(shift_hbm, shift_ref, small_sems.at[1]),
    ]
    table_copies = [
        pltpu.make_async_copy(high_hbm, table_hi, small_sems.at[2]),
        pltpu.make_async_copy(low_hbm, table_lo, small_sems.at[3]),
    ]
    frame_copies = [
        pltpu.make_async_copy(
            ref.at[:, pl.ds(g * LANES, LANES)],
            frame.at[2 * g + 1, pl.ds(row, rows), :],
            frame_sems.at[n, g],
        )
        for n, (ref, row, rows) in enumerate(
            ((second_hbm, HALO, band), (top_hbm, 0, HALO), (bottom_hbm, HALO + band, HALO))
        )
        for g in range(tiles)
    ]
    for copy in small_copies + frame_copies + table_copies:
        copy.start()

    for copy in small_copies:
        copy.wait()
    for axis in range(2):
        for a, values in enumerate(cubic_weights(fraction_ref[axis, :, 0, :])):
            taps_vmem[2 * a + axis, 0:5, 0:80] = values
    taps_copy = pltpu.make_async_copy(taps_vmem, taps_ref, small_sems.at[4])
    taps_copy.start()

    for copy in frame_copies:
        copy.wait()
    wide = lax.broadcasted_iota(jnp.int32, (16, LANES), 1) < 64

    def fill(step, carry):
        rows = pl.ds(pl.multiple_of(step * 16, 16), 16)
        before = before_turned = jnp.zeros((16, LANES), jnp.float32)
        for g in range(tiles):
            here = frame[2 * g + 1, rows, :]
            turned = pltpu.roll(here, 64, 1)
            swapped[2 * g + 1, rows, :] = turned
            frame[2 * g, rows, :] = jnp.where(wide, before_turned, turned)
            swapped[2 * g, rows, :] = jnp.where(wide, here, before)
            before, before_turned = here, turned
        frame[2 * tiles, rows, :] = jnp.where(wide, before_turned, 0.0)
        swapped[2 * tiles, rows, :] = jnp.where(wide, 0.0, before)
        return carry

    lax.fori_loop(0, frame.shape[1] // 16, fill, 0)
    taps_copy.wait()

    def mix_rows(step, k):
        i, column = step >> 3, (step & 7) * 10 + k
        start = i * WIN + (HALO - 1) + shift_ref[0, i, 0, column]
        tile = (step & 7) * 5 + (k + 1) // 2
        base = (64, 32)[k % 2]
        turn = 257 - base - shift_ref[1, i, 0, column]
        ry = [taps_ref[2 * a, i, column] for a in range(4)]
        inside = (lane >= base - 16) & (lane < base + 48)
        rows = [frame[tile, pl.ds(start + m, 8, stride=4), :] for m in range(5)]
        others = [swapped[tile, pl.ds(start + 2 + m, 8, stride=4), :] for m in range(5)]
        mixed = []
        for j in range(2):
            one = (ry[0] * rows[j] + ry[1] * rows[j + 1]) + (ry[2] * rows[j + 2] + ry[3] * rows[j + 3])
            two = (ry[0] * others[j] + ry[1] * others[j + 1]) + (ry[2] * others[j + 2] + ry[3] * others[j + 3])
            mixed.append(pltpu.roll(jnp.where(inside, one, two), (turn + 32 * j) & 127, 1))
        shifted[k, 0] = jnp.where(even, mixed[0], mixed[1])
        shifted[k, 1] = jnp.where(even, mixed[1], mixed[0])

    def mix_columns(step, k, base):
        i, column = step >> 3, (step & 7) * 10 + k
        rx = [taps_ref[2 * a + 1, i, column] for a in range(4)]
        one, following = shifted[k, 0], shifted[k, 1]
        total = rx[0] * one
        for b in range(1, 4):
            total = total + rx[b] * pltpu.roll(jnp.where((lane & 31) < b, following, one), LANES - b, 1)
        second_win[pl.ds(pl.multiple_of(base[k // 5] + (k % 5) * 8, 8), 8), :] = total

    steps = 8 * win_rows
    for k in range(10):
        mix_rows(0, k)

    def deform(step, carry):
        base = [place(step & 7, core, step >> 3, block) for core in range(2)]
        later = jnp.minimum(step + 1, steps - 1)
        for k in range(10):
            mix_columns(step, k, base)
            mix_rows(later, k)
        return carry

    lax.fori_loop(0, steps, deform, 0)

    def finish(at, power):
        scale = (2.0 / (1024.0 * 1024.0)) / jnp.sqrt(power_ref[at, :] * power)
        powers[at, :] = scale

    lift_windows(second_win, pair_ends, pair_hi, pair_lo, finish)
    for copy in table_copies:
        copy.wait()

    for unit in range(5):
        second = spectrum_of(unit, pair_ends, pair_hi, pair_lo, table_hi, table_lo)
        fr, fi = spectra_ref[unit, :, :LANES], spectra_ref[unit, :, LANES:]
        sr, si = second[:, :LANES], second[:, LANES:]
        re_hi, re_lo = split(fr * sr + fi * si)
        im_hi, im_lo = split(fr * si - fi * sr)
        high = jnp.concatenate([re_hi, im_hi], axis=1)
        low = jnp.concatenate([re_lo, im_lo], axis=1)
        rows = LANES if unit < 2 else 2 * LANES
        hi, lo = table_hi[unit, 0:rows], table_lo[unit, 0:rows]
        result = dot_back(high, hi) + dot_back(low, hi) + dot_back(high, lo)
        if unit < 2:
            back[unit] = result
        else:
            back[2 * unit - 2] = result[:, :LANES]
            back[2 * unit - 1] = result[:, LANES:]

    for part, out_ref in enumerate((away_ref, keep_ref)):

        def lower(step, carry, out_ref=out_ref, offset=(1 - part) * (windows // 2)):
            at = pl.ds(pl.multiple_of(offset + step * 8, 8), 8)
            b0, b4, b1r, b1i, b2r, b2i, b3r, b3i = (back[u, at, :] for u in range(8))
            scale = powers[at, :]
            plus, minus = (b0 + b4) * 0.5, (b0 - b4) * 0.5
            evens = (plus + b2r, minus - b2i, plus - b2r, minus + b2i)
            u, v = (b1r - b3r) * ROOT_HALF, (b1i + b3i) * ROOT_HALF
            odds = (b1r + b3r, u - v, b3i - b1i, -(u + v))
            for l in range(4):
                out_ref[pl.ds(step * 64 + l, 8, stride=8), :] = 1.0 + (evens[l] + odds[l]) * scale
                out_ref[pl.ds(step * 64 + l + 4, 8, stride=8), :] = 1.0 + (evens[l] - odds[l]) * scale
            return carry

        lax.fori_loop(0, windows // 16, lower, 0, unroll=5)


def band_planes(shifts, fractions, first, second, top, bottom):
    windows = first.shape[0] * first.shape[1] // (WIN * WIN)
    tiles = first.shape[1] // LANES
    tall = first.shape[0] + 2 * HALO

    def pinned(array):
        return pltpu.with_memory_space_constraint(array, pltpu.HBM)

    first, second, *tables = map(pinned, (first, second, *(jnp.asarray(t) for t in dft_tables())))
    vmem = pl.BlockSpec(memory_space=pltpu.VMEM)
    hbm = pl.BlockSpec(memory_space=pltpu.HBM)
    either = pl.BlockSpec(memory_space=pl.ANY)
    f32, bf16 = jnp.float32, jnp.bfloat16
    half = jax.ShapeDtypeStruct((windows * 4, LANES), f32)
    pairs = [
        pltpu.VMEM((2, windows, 2 * LANES), bf16),
        pltpu.VMEM((3, windows, 2 * LANES), bf16),
        pltpu.VMEM((3, windows, 2 * LANES), bf16),
    ]
    held = [pltpu.VMEM(t.shape, bf16) for t in tables]
    spectra, powers = pl.pallas_call(
        first_kernel,
        out_shape=[
            jax.ShapeDtypeStruct((5, windows, 2 * LANES), f32),
            jax.ShapeDtypeStruct((windows, LANES), f32),
        ],
        in_specs=[hbm, hbm, hbm],
        out_specs=[vmem, vmem],
        scratch_shapes=[
            pltpu.VMEM((tiles, first.shape[0], LANES), f32),
            pltpu.VMEM((windows * 8, LANES), f32),
            *pairs,
            *held,
            pltpu.SemaphoreType.DMA((tiles,)),
            pltpu.SemaphoreType.DMA((2,)),
        ],
        compiler_params=pltpu.CompilerParams(vmem_limit_bytes=30 * 1024 * 1024),
        cost_estimate=pl.CostEstimate(flops=10**10, bytes_accessed=2 * 10**7, transcendentals=0),
        name="first_spectra",
    )(first, *tables)
    row_shape = (2, 5, 1, 80)
    return pl.pallas_call(
        band_kernel,
        out_shape=[half, half],
        in_specs=[hbm, hbm, hbm, either, either, hbm, hbm, vmem, vmem],
        out_specs=[vmem, vmem],
        scratch_shapes=[
            pltpu.VMEM((2 * tiles + 1, tall, LANES), f32),
            pltpu.VMEM((2 * tiles + 1, tall, LANES), f32),
            pltpu.VMEM((10, 2, 8, LANES), f32),
            pltpu.VMEM((windows * 8, LANES), f32),
            *pairs,
            pltpu.VMEM((windows, LANES), f32),
            pltpu.VMEM((8, windows, LANES), f32),
            pltpu.VMEM(row_shape, f32),
            pltpu.SMEM(row_shape, jnp.int32),
            pltpu.VMEM((8, 8, LANES), f32),
            pltpu.SMEM((8, 8, LANES), f32),
            *held,
            pltpu.SemaphoreType.DMA((3, tiles)),
            pltpu.SemaphoreType.DMA((5,)),
        ],
        compiler_params=pltpu.CompilerParams(vmem_limit_bytes=40 * 1024 * 1024),
        name="band_planes",
    )(pinned(jnp.swapaxes(shifts, 1, 2)), pinned(jnp.swapaxes(fractions, 1, 2)), second, top, bottom, *tables,
      spectra, powers)


def along_z(array, hops):
    pairs = [(2 * z + c, 2 * ((z + (hops, -hops)[c]) % 8) + c) for z in range(8) for c in range(2)]
    return lax.ppermute(array, "sep", pairs)


def reduced(keep, away):
    size = keep.shape[0] // 8
    parts = keep * lax.ppermute(away, "sep", [(s, s ^ 1) for s in range(16)])
    ahead = along_z(parts[3 * size : 5 * size], 1)
    behind = along_z(parts[5 * size :], -1)
    near = parts[: 3 * size] * behind
    third = along_z(near[size : 2 * size] * ahead[size:], 3)
    sixth = along_z(near[2 * size :], -2)
    return near[:size] * ahead[:size] * third * sixth


def local(first, seconds, shifts, fractions):
    second = seconds[0]
    top = lax.ppermute(second[-HALO:], "tile", [(i, i + 1) for i in range(15)])
    bottom = lax.ppermute(second[:HALO], "tile", [(i + 1, i) for i in range(15)])
    planes = band_planes(shifts, fractions, first, second, top, bottom)
    return reduced(*planes).reshape(5, 5, 1024)


def solution(mesh):
    in_specs = (
        P("tile", None),
        P("sep", "tile", None),
        P(None, "sep", "tile", None),
        P(None, "sep", "tile", None),
    )
    out_specs = P("tile", "sep", None)
    return jax.shard_map(local, mesh=mesh, in_specs=in_specs, out_specs=out_specs, check_vma=False)
```

```python
import functools
import math

import jax
import jax.numpy as jnp
import ml_dtypes
import numpy as np
from jax import lax
from jax.experimental import pallas as pl
from jax.experimental.pallas import tpu as pltpu
from jax.sharding import PartitionSpec as P

WIN = 32
HALO = 16
EPS = 1e-06
LANES = 128
BLOCKS = 16
ROOT_HALF = math.sqrt(0.5)


def split_table(table):
    high = table.astype(ml_dtypes.bfloat16)
    low = (table - high.astype(np.float64)).astype(ml_dtypes.bfloat16)
    return high, low


def dft_tables():
    major, minor = np.divmod(np.arange(LANES), WIN)
    high, low = [], []
    for unit in (0, 4, 1, 2, 3):
        phase = (np.outer(major, unit + 8 * major) + np.outer(minor, minor)) % WIN
        cos = np.cos(phase * (2.0 * np.pi / WIN))
        sin = np.sin(phase * (2.0 * np.pi / WIN))
        if unit in (0, 4):
            table = np.concatenate([np.concatenate([cos, -sin], axis=1)] * 2)
        else:
            table = np.block([[cos, -sin], [sin, cos]])
        high.append(split_table(table)[0])
        low.append(split_table(table)[1])
    return np.stack(high), np.stack(low)


def split(value):
    high = value.astype(jnp.bfloat16)
    return high, (value - high.astype(jnp.float32)).astype(jnp.bfloat16)


def dot(left, right):
    return jnp.dot(left, right, preferred_element_type=jnp.float32)


def dot_back(left, right):
    return lax.dot_general(left, right, (((1,), (1,)), ((), ())), preferred_element_type=jnp.float32)


def cubic_weights(fraction):
    squared = fraction * fraction
    cubed = squared * fraction
    return (
        -0.5 * cubed + squared - 0.5 * fraction,
        1.5 * cubed - 2.5 * squared + 1.0,
        -1.5 * cubed + 2.0 * squared + 0.5 * fraction,
        0.5 * cubed - 0.5 * squared,
    )


def masks():
    lane = lax.broadcasted_iota(jnp.int32, (8, LANES), 1)
    return lane, lane < 64, (lane % 64) < 32


def place(chip, core, i, block):
    own = lax.axis_index("sep")
    own_chip, own_core = own >> 1, own & 1
    turn = chip - own_chip if core == 0 else own_chip - chip
    return ((((own_core ^ core) * 8 + ((3 * turn) & 7)) * block) + i * 5) * 8


def lift_windows(source, pair_ends, pair_hi, pair_lo, finish):
    def lift(step, carry):
        at = pl.ds(pl.multiple_of(step * 16, 16), 16)
        x = [source[pl.ds(step * 128 + l, 16, stride=8), :] for l in range(8)]
        total = ((x[0] + x[1]) + (x[2] + x[3])) + ((x[4] + x[5]) + (x[6] + x[7]))
        mean = jnp.sum(total, axis=1, keepdims=True) * (1.0 / 1024.0)
        x = [v - mean for v in x]
        q = [v * v for v in x]
        total = ((q[0] + q[1]) + (q[2] + q[3])) + ((q[4] + q[5]) + (q[6] + q[7]))
        finish(at, jnp.sum(total, axis=1, keepdims=True) * (1.0 / 1024.0) + EPS)
        s = [x[l] + x[l + 4] for l in range(4)]
        d = [x[l] - x[l + 4] for l in range(4)]
        e, o = s[0] + s[2], s[1] + s[3]
        p, m = (d[1] + d[3]) * ROOT_HALF, (d[1] - d[3]) * ROOT_HALF
        for unit, value in enumerate((e + o, e - o)):
            high, low = split(value)
            pair_ends[unit, at, 0:LANES] = high
            pair_ends[unit, at, LANES : 2 * LANES] = low
        mids = ((d[0] + m, -(d[2] + p)), (s[0] - s[2], s[3] - s[1]), (d[0] - m, d[2] - p))
        for unit, parts in enumerate(mids):
            for half, value in enumerate(parts):
                high, low = split(value)
                pair_hi[unit, at, half * LANES : (half + 1) * LANES] = high
                pair_lo[unit, at, half * LANES : (half + 1) * LANES] = low
        return carry

    lax.fori_loop(0, source.shape[0] // 128, lift, 0, unroll=5)


def spectrum_of(unit, pair_ends, pair_hi, pair_lo, table_hi, table_lo):
    hi, lo = table_hi[unit], table_lo[unit]
    if unit < 2:
        return dot(pair_ends[unit], hi) + dot(pair_ends[unit, :, 0:LANES], lo[0:LANES])
    return dot(pair_hi[unit - 2], hi) + dot(pair_lo[unit - 2], hi) + dot(pair_hi[unit - 2], lo)


def first_kernel(fraction_hbm, first_hbm, high_hbm, low_hbm, spectra_ref, power_ref, taps_ref, fraction_ref,
                 first, first_win, pair_ends, pair_hi, pair_lo, table_hi, table_lo, first_sems, table_sems):
    win_rows = first_hbm.shape[0] // WIN
    block = first_win.shape[0] // 8 // BLOCKS
    lane, low_half, even = masks()
    outer_blocks = (lane < 32) | (lane >= 96)
    first_copies = [
        pltpu.make_async_copy(first_hbm.at[:, pl.ds(g * LANES, LANES)], first.at[g], first_sems.at[g])
        for g in range(first.shape[0])
    ]
    table_copies = [
        pltpu.make_async_copy(high_hbm, table_hi, table_sems.at[0]),
        pltpu.make_async_copy(low_hbm, table_lo, table_sems.at[1]),
        pltpu.make_async_copy(fraction_hbm, fraction_ref, table_sems.at[2]),
    ]
    for copy in first_copies + table_copies:
        copy.start()
    taps_ref[...] = jnp.zeros_like(taps_ref)
    for copy in first_copies:
        copy.wait()

    def gather(step, carry):
        i, quarter = step >> 2, step & 3
        base = [place(quarter * 2 + (n >> 1), n & 1, i, block) for n in range(4)]
        for g in range(5):
            v = [first[quarter * 5 + g, pl.ds(i * WIN + j, 8, stride=4), :] for j in range(4)]
            turned = pltpu.roll(jnp.where(outer_blocks, v[2], v[0]), 64, 1)
            p = jnp.where(low_half, jnp.where(even, v[0], v[2]), turned)
            q = jnp.where(low_half, turned, jnp.where(even, v[2], v[0]))
            turned = pltpu.roll(jnp.where(low_half, v[3], v[1]), 64, 1)
            r = jnp.where(low_half, v[1], turned)
            s = jnp.where(low_half, turned, v[3])
            for w, (one, two) in ((0, (p, r)), (2, (q, s))):
                turned = pltpu.roll(jnp.where(even, two, one), 32, 1)
                for k, value in (
                    (4 * g + w, jnp.where(even, one, turned)),
                    (4 * g + w + 1, jnp.where(even, turned, two)),
                ):
                    first_win[pl.ds(pl.multiple_of(base[k // 5] + (k % 5) * 8, 8), 8), :] = value
        return carry

    lax.fori_loop(0, 4 * win_rows, gather, 0, unroll=4)


    def finish(at, power):
        power_ref[at, :] = jnp.broadcast_to(power, (16, LANES))

    lift_windows(first_win, pair_ends, pair_hi, pair_lo, finish)
    for copy in table_copies:
        copy.wait()
    for axis in range(2):
        for a, values in enumerate(cubic_weights(fraction_ref[axis, :, 0, :])):
            taps_ref[2 * a + axis, 0:5, 0:80] = values
    for unit in range(5):
        spectra_ref[unit] = spectrum_of(unit, pair_ends, pair_hi, pair_lo, table_hi, table_lo)


def band_kernel(shift_hbm, taps_vmem, second_ref, top_ref, bottom_ref, high_hbm, low_hbm, spectra_ref, power_ref,
                keep_ref, away_ref, frame, swapped, shifted, second_win,
                pair_ends, pair_hi, pair_lo, powers, back, shift_ref, taps_ref, table_hi, table_lo, small_sems):
    windows = second_win.shape[0] // 8
    band = second_ref.shape[0]
    win_rows = band // WIN
    block = windows // BLOCKS
    tiles = second_ref.shape[1] // LANES
    lane, low_half, even = masks()

    small_copies = [
        pltpu.make_async_copy(taps_vmem, taps_ref, small_sems.at[0]),
        pltpu.make_async_copy(shift_hbm, shift_ref, small_sems.at[1]),
    ]
    table_copies = [
        pltpu.make_async_copy(high_hbm, table_hi, small_sems.at[2]),
        pltpu.make_async_copy(low_hbm, table_lo, small_sems.at[3]),
    ]
    for copy in small_copies + table_copies:
        copy.start()

    wide = lax.broadcasted_iota(jnp.int32, (16, LANES), 1) < 64

    def fill(source, source_row, row):
        rows = pl.ds(pl.multiple_of(row, 16), 16)
        before = before_turned = jnp.zeros((16, LANES), jnp.float32)
        for g in range(tiles):
            here = source[pl.ds(pl.multiple_of(source_row, 16), 16), g * LANES : (g + 1) * LANES]
            turned = pltpu.roll(here, 64, 1)
            frame[2 * g + 1, rows, :] = here
            swapped[2 * g + 1, rows, :] = turned
            frame[2 * g, rows, :] = jnp.where(wide, before_turned, turned)
            swapped[2 * g, rows, :] = jnp.where(wide, here, before)
            before, before_turned = here, turned
        frame[2 * tiles, rows, :] = jnp.where(wide, before_turned, 0.0)
        swapped[2 * tiles, rows, :] = jnp.where(wide, 0.0, before)

    def fill_band(step, carry):
        fill(second_ref, step * 16, step * 16 + HALO)
        return carry

    fill(top_ref, 0, 0)
    fill(bottom_ref, 0, HALO + band)
    lax.fori_loop(0, band // 16, fill_band, 0, unroll=2)
    for copy in small_copies:
        copy.wait()

    def mix_rows(step, k):
        i, column = step >> 3, (step & 7) * 10 + k
        start = i * WIN + (HALO - 1) + shift_ref[0, i, 0, column]
        tile = (step & 7) * 5 + (k + 1) // 2
        base = (64, 32)[k % 2]
        turn = 257 - base - shift_ref[1, i, 0, column]
        ry = [taps_ref[2 * a, i, column] for a in range(4)]
        inside = (lane >= base - 16) & (lane < base + 48)
        rows = [frame[tile, pl.ds(start + m, 8, stride=4), :] for m in range(5)]
        others = [swapped[tile, pl.ds(start + 2 + m, 8, stride=4), :] for m in range(5)]
        mixed = []
        for j in range(2):
            one = (ry[0] * rows[j] + ry[1] * rows[j + 1]) + (ry[2] * rows[j + 2] + ry[3] * rows[j + 3])
            two = (ry[0] * others[j] + ry[1] * others[j + 1]) + (ry[2] * others[j + 2] + ry[3] * others[j + 3])
            mixed.append(pltpu.roll(jnp.where(inside, one, two), (turn + 32 * j) & 127, 1))
        shifted[k, 0] = jnp.where(even, mixed[0], mixed[1])
        shifted[k, 1] = jnp.where(even, mixed[1], mixed[0])

    def mix_columns(step, k, base):
        i, column = step >> 3, (step & 7) * 10 + k
        rx = [taps_ref[2 * a + 1, i, column] for a in range(4)]
        one, following = shifted[k, 0], shifted[k, 1]
        total = rx[0] * one
        for b in range(1, 4):
            total = total + rx[b] * pltpu.roll(jnp.where((lane & 31) < b, following, one), LANES - b, 1)
        second_win[pl.ds(pl.multiple_of(base[k // 5] + (k % 5) * 8, 8), 8), :] = total

    steps = 8 * win_rows
    for k in range(10):
        mix_rows(0, k)

    def deform(step, carry):
        base = [place(step & 7, core, step >> 3, block) for core in range(2)]
        later = jnp.minimum(step + 1, steps - 1)
        for k in range(10):
            mix_columns(step, k, base)
            mix_rows(later, k)
        return carry

    lax.fori_loop(0, steps, deform, 0, unroll=2)

    def finish(at, power):
        scale = (2.0 / (1024.0 * 1024.0)) / jnp.sqrt(power_ref[at, :] * power)
        powers[at, :] = scale

    lift_windows(second_win, pair_ends, pair_hi, pair_lo, finish)
    for copy in table_copies:
        copy.wait()

    for unit in range(5):
        second = spectrum_of(unit, pair_ends, pair_hi, pair_lo, table_hi, table_lo)
        fr, fi = spectra_ref[unit, :, :LANES], spectra_ref[unit, :, LANES:]
        sr, si = second[:, :LANES], second[:, LANES:]
        re_hi, re_lo = split(fr * sr + fi * si)
        im_hi, im_lo = split(fr * si - fi * sr)
        high = jnp.concatenate([re_hi, im_hi], axis=1)
        low = jnp.concatenate([re_lo, im_lo], axis=1)
        rows = LANES if unit < 2 else 2 * LANES
        hi, lo = table_hi[unit, 0:rows], table_lo[unit, 0:rows]
        result = dot_back(high, hi) + dot_back(low, hi) + dot_back(high, lo)
        if unit < 2:
            back[unit] = result
        else:
            back[2 * unit - 2] = result[:, :LANES]
            back[2 * unit - 1] = result[:, LANES:]

    for part, out_ref in enumerate((away_ref, keep_ref)):

        def lower(step, carry, out_ref=out_ref, offset=(1 - part) * (windows // 2)):
            at = pl.ds(pl.multiple_of(offset + step * 8, 8), 8)
            b0, b4, b1r, b1i, b2r, b2i, b3r, b3i = (back[u, at, :] for u in range(8))
            scale = powers[at, :]
            plus, minus = (b0 + b4) * 0.5, (b0 - b4) * 0.5
            evens = (plus + b2r, minus - b2i, plus - b2r, minus + b2i)
            u, v = (b1r - b3r) * ROOT_HALF, (b1i + b3i) * ROOT_HALF
            odds = (b1r + b3r, u - v, b3i - b1i, -(u + v))
            for l in range(4):
                out_ref[pl.ds(step * 64 + l, 8, stride=8), :] = 1.0 + (evens[l] + odds[l]) * scale
                out_ref[pl.ds(step * 64 + l + 4, 8, stride=8), :] = 1.0 + (evens[l] - odds[l]) * scale
            return carry

        lax.fori_loop(0, windows // 16, lower, 0, unroll=5)


def band_planes(shifts, fractions, first, second, top, bottom):
    windows = first.shape[0] * first.shape[1] // (WIN * WIN)
    tiles = first.shape[1] // LANES
    tall = first.shape[0] + 2 * HALO

    def pinned(array):
        return pltpu.with_memory_space_constraint(array, pltpu.HBM)

    tables = [jnp.asarray(t) for t in dft_tables()]
    vmem = pl.BlockSpec(memory_space=pltpu.VMEM)
    hbm = pl.BlockSpec(memory_space=pltpu.HBM)
    f32, bf16 = jnp.float32, jnp.bfloat16
    half = jax.ShapeDtypeStruct((windows * 4, LANES), f32)
    pairs = [
        pltpu.VMEM((2, windows, 2 * LANES), bf16),
        pltpu.VMEM((3, windows, 2 * LANES), bf16),
        pltpu.VMEM((3, windows, 2 * LANES), bf16),
    ]
    held = [pltpu.VMEM(t.shape, bf16) for t in tables]
    row_shape = (2, 5, 1, 80)
    spectra, powers, taps = pl.pallas_call(
        first_kernel,
        out_shape=[
            jax.ShapeDtypeStruct((5, windows, 2 * LANES), f32),
            jax.ShapeDtypeStruct((windows, LANES), f32),
            jax.ShapeDtypeStruct((8, 8, LANES), f32),
        ],
        in_specs=[hbm, hbm, hbm, hbm],
        out_specs=[vmem, vmem, vmem],
        scratch_shapes=[
            pltpu.VMEM(row_shape, f32),
            pltpu.VMEM((tiles, first.shape[0], LANES), f32),
            pltpu.VMEM((windows * 8, LANES), f32),
            *pairs,
            *held,
            pltpu.SemaphoreType.DMA((tiles,)),
            pltpu.SemaphoreType.DMA((3,)),
        ],
        compiler_params=pltpu.CompilerParams(vmem_limit_bytes=30 * 1024 * 1024),
        cost_estimate=pl.CostEstimate(flops=10**10, bytes_accessed=2 * 10**7, transcendentals=0),
        name="first_spectra",
    )(pinned(jnp.swapaxes(fractions, 1, 2)), pinned(first), *map(pinned, tables))
    return pl.pallas_call(
        band_kernel,
        out_shape=[half, half],
        in_specs=[hbm, vmem, vmem, vmem, vmem, hbm, hbm, vmem, vmem],
        out_specs=[vmem, vmem],
        scratch_shapes=[
            pltpu.VMEM((2 * tiles + 1, tall, LANES), f32),
            pltpu.VMEM((2 * tiles + 1, tall, LANES), f32),
            pltpu.VMEM((10, 2, 8, LANES), f32),
            pltpu.VMEM((windows * 8, LANES), f32),
            *pairs,
            pltpu.VMEM((windows, LANES), f32),
            pltpu.VMEM((8, windows, LANES), f32),
            pltpu.SMEM(row_shape, jnp.int32),
            pltpu.SMEM((8, 8, LANES), f32),
            *held,
            pltpu.SemaphoreType.DMA((4,)),
        ],
        compiler_params=pltpu.CompilerParams(vmem_limit_bytes=40 * 1024 * 1024),
        name="band_planes",
    )(pinned(jnp.swapaxes(shifts, 1, 2)), taps, second, top, bottom,
      *map(pinned, tables), spectra, powers)


def along_z(array, hops):
    pairs = [(2 * z + c, 2 * ((z + (hops, -hops)[c]) % 8) + c) for z in range(8) for c in range(2)]
    return lax.ppermute(array, "sep", pairs)


def reduced(keep, away):
    size = keep.shape[0] // 8
    parts = keep * lax.ppermute(away, "sep", [(s, s ^ 1) for s in range(16)])
    ahead = along_z(parts[3 * size : 5 * size], 1)
    behind = along_z(parts[5 * size :], -1)
    near = parts[: 3 * size] * behind
    third = along_z(near[size : 2 * size] * ahead[size:], 3)
    sixth = along_z(near[2 * size :], -2)
    return near[:size] * ahead[:size] * third * sixth


def local(first, seconds, shifts, fractions):
    second = seconds[0]
    top = lax.ppermute(second[-HALO:], "tile", [(i, i + 1) for i in range(15)])
    bottom = lax.ppermute(second[:HALO], "tile", [(i + 1, i) for i in range(15)])
    planes = band_planes(shifts, fractions, first, second, top, bottom)
    return reduced(*planes).reshape(5, 5, 1024)


def solution(mesh):
    in_specs = (
        P("tile", None),
        P("sep", "tile", None),
        P(None, "sep", "tile", None),
        P(None, "sep", "tile", None),
    )
    out_specs = P("tile", "sep", None)
    return jax.shard_map(local, mesh=mesh, in_specs=in_specs, out_specs=out_specs, check_vma=False)
```

```python
import functools
import math

import jax
import jax.numpy as jnp
import ml_dtypes
import numpy as np
from jax import lax
from jax.experimental import pallas as pl
from jax.experimental.pallas import tpu as pltpu
from jax.sharding import PartitionSpec as P

WIN = 32
HALO = 16
SENT = 10
EPS = 1e-06
LANES = 128
BLOCKS = 16
ROOT_HALF = math.sqrt(0.5)


def split_table(table):
    high = table.astype(ml_dtypes.bfloat16)
    low = (table - high.astype(np.float64)).astype(ml_dtypes.bfloat16)
    return high, low


def dft_tables():
    major, minor = np.divmod(np.arange(LANES), WIN)
    high, low = [], []
    for unit in (0, 4, 1, 2, 3):
        phase = (np.outer(major, unit + 8 * major) + np.outer(minor, minor)) % WIN
        cos = np.cos(phase * (2.0 * np.pi / WIN))
        sin = np.sin(phase * (2.0 * np.pi / WIN))
        if unit in (0, 4):
            table = np.concatenate([np.concatenate([cos, -sin], axis=1)] * 2)
        else:
            table = np.block([[cos, -sin], [sin, cos]])
        high.append(split_table(table)[0])
        low.append(split_table(table)[1])
    return np.stack(high), np.stack(low)


def split(value):
    high = value.astype(jnp.bfloat16)
    return high, (value - high.astype(jnp.float32)).astype(jnp.bfloat16)


def dot(left, right):
    return jnp.dot(left, right, preferred_element_type=jnp.float32)


def dot_back(left, right):
    return lax.dot_general(left, right, (((1,), (1,)), ((), ())), preferred_element_type=jnp.float32)


def cubic_weights(fraction):
    squared = fraction * fraction
    cubed = squared * fraction
    return (
        -0.5 * cubed + squared - 0.5 * fraction,
        1.5 * cubed - 2.5 * squared + 1.0,
        -1.5 * cubed + 2.0 * squared + 0.5 * fraction,
        0.5 * cubed - 0.5 * squared,
    )


def masks():
    lane = lax.broadcasted_iota(jnp.int32, (8, LANES), 1)
    return lane, lane < 64, (lane % 64) < 32


def place(chip, core, i, block):
    own = lax.axis_index("sep")
    own_chip, own_core = own >> 1, own & 1
    turn = chip - own_chip if core == 0 else own_chip - chip
    return ((((own_core ^ core) * 8 + ((3 * turn) & 7)) * block) + i * 5) * 8


def lift_windows(source, pair_ends, pair_hi, pair_lo, finish):
    def lift(step, carry):
        at = pl.ds(pl.multiple_of(step * 16, 16), 16)
        x = [source[pl.ds(step * 128 + l, 16, stride=8), :] for l in range(8)]
        total = ((x[0] + x[1]) + (x[2] + x[3])) + ((x[4] + x[5]) + (x[6] + x[7]))
        mean = jnp.sum(total, axis=1, keepdims=True) * (1.0 / 1024.0)
        x = [v - mean for v in x]
        q = [v * v for v in x]
        total = ((q[0] + q[1]) + (q[2] + q[3])) + ((q[4] + q[5]) + (q[6] + q[7]))
        finish(at, jnp.sum(total, axis=1, keepdims=True) * (1.0 / 1024.0) + EPS)
        s = [x[l] + x[l + 4] for l in range(4)]
        d = [x[l] - x[l + 4] for l in range(4)]
        e, o = s[0] + s[2], s[1] + s[3]
        p, m = (d[1] + d[3]) * ROOT_HALF, (d[1] - d[3]) * ROOT_HALF
        for unit, value in enumerate((e + o, e - o)):
            high, low = split(value)
            pair_ends[unit, at, 0:LANES] = high
            pair_ends[unit, at, LANES : 2 * LANES] = low
        mids = ((d[0] + m, -(d[2] + p)), (s[0] - s[2], s[3] - s[1]), (d[0] - m, d[2] - p))
        for unit, parts in enumerate(mids):
            for half, value in enumerate(parts):
                high, low = split(value)
                pair_hi[unit, at, half * LANES : (half + 1) * LANES] = high
                pair_lo[unit, at, half * LANES : (half + 1) * LANES] = low
        return carry

    lax.fori_loop(0, source.shape[0] // 128, lift, 0, unroll=5)


def spectrum_of(unit, pair_ends, pair_hi, pair_lo, table_hi, table_lo):
    hi, lo = table_hi[unit], table_lo[unit]
    if unit < 2:
        return dot(pair_ends[unit], hi) + dot(pair_ends[unit, :, 0:LANES], lo[0:LANES])
    return dot(pair_hi[unit - 2], hi) + dot(pair_lo[unit - 2], hi) + dot(pair_hi[unit - 2], lo)


def first_kernel(fraction_hbm, first_hbm, high_hbm, low_hbm, spectra_ref, power_ref, taps_ref, fraction_ref,
                 first, first_win, pair_ends, pair_hi, pair_lo, table_hi, table_lo, first_sems, table_sems):
    win_rows = first_hbm.shape[0] // WIN
    block = first_win.shape[0] // 8 // BLOCKS
    lane, low_half, even = masks()
    outer_blocks = (lane < 32) | (lane >= 96)
    first_copies = [
        pltpu.make_async_copy(first_hbm.at[:, pl.ds(g * LANES, LANES)], first.at[g], first_sems.at[g])
        for g in range(first.shape[0])
    ]
    table_copies = [
        pltpu.make_async_copy(high_hbm, table_hi, table_sems.at[0]),
        pltpu.make_async_copy(low_hbm, table_lo, table_sems.at[1]),
        pltpu.make_async_copy(fraction_hbm, fraction_ref, table_sems.at[2]),
    ]
    for copy in first_copies + table_copies:
        copy.start()
    taps_ref[...] = jnp.zeros_like(taps_ref)
    for copy in first_copies:
        copy.wait()

    def gather(step, carry):
        i, quarter = step >> 2, step & 3
        base = [place(quarter * 2 + (n >> 1), n & 1, i, block) for n in range(4)]
        for g in range(5):
            v = [first[quarter * 5 + g, pl.ds(i * WIN + j, 8, stride=4), :] for j in range(4)]
            turned = pltpu.roll(jnp.where(outer_blocks, v[2], v[0]), 64, 1)
            p = jnp.where(low_half, jnp.where(even, v[0], v[2]), turned)
            q = jnp.where(low_half, turned, jnp.where(even, v[2], v[0]))
            turned = pltpu.roll(jnp.where(low_half, v[3], v[1]), 64, 1)
            r = jnp.where(low_half, v[1], turned)
            s = jnp.where(low_half, turned, v[3])
            for w, (one, two) in ((0, (p, r)), (2, (q, s))):
                turned = pltpu.roll(jnp.where(even, two, one), 32, 1)
                for k, value in (
                    (4 * g + w, jnp.where(even, one, turned)),
                    (4 * g + w + 1, jnp.where(even, turned, two)),
                ):
                    first_win[pl.ds(pl.multiple_of(base[k // 5] + (k % 5) * 8, 8), 8), :] = value
        return carry

    lax.fori_loop(0, 4 * win_rows, gather, 0, unroll=4)


    def finish(at, power):
        power_ref[at, :] = jnp.broadcast_to(power, (16, LANES))

    lift_windows(first_win, pair_ends, pair_hi, pair_lo, finish)
    for copy in table_copies:
        copy.wait()
    for axis in range(2):
        for a, values in enumerate(cubic_weights(fraction_ref[axis, :, 0, :])):
            taps_ref[2 * a + axis, 0:5, 0:80] = values
    for unit in range(5):
        spectra_ref[unit] = spectrum_of(unit, pair_ends, pair_hi, pair_lo, table_hi, table_lo)


def band_kernel(shift_hbm, taps_vmem, second_ref, top_ref, bottom_ref, high_hbm, low_hbm, spectra_ref, power_ref,
                keep_ref, away_ref, frame, swapped, shifted, second_win,
                pair_ends, pair_hi, pair_lo, powers, back, shift_ref, taps_ref, table_hi, table_lo, small_sems):
    windows = second_win.shape[0] // 8
    band = second_ref.shape[0]
    win_rows = band // WIN
    block = windows // BLOCKS
    tiles = second_ref.shape[1] // LANES
    lane, low_half, even = masks()

    small_copies = [
        pltpu.make_async_copy(taps_vmem, taps_ref, small_sems.at[0]),
        pltpu.make_async_copy(shift_hbm, shift_ref, small_sems.at[1]),
    ]
    table_copies = [
        pltpu.make_async_copy(high_hbm, table_hi, small_sems.at[2]),
        pltpu.make_async_copy(low_hbm, table_lo, small_sems.at[3]),
    ]
    for copy in small_copies + table_copies:
        copy.start()

    def fill(source, source_rows, rows):
        wide = lax.broadcasted_iota(jnp.int32, (rows.size, LANES), 1) < 64
        before = before_turned = jnp.zeros((rows.size, LANES), jnp.float32)
        for g in range(tiles):
            here = source[source_rows, g * LANES : (g + 1) * LANES]
            turned = pltpu.roll(here, 64, 1)
            frame[2 * g + 1, rows, :] = here
            swapped[2 * g + 1, rows, :] = turned
            frame[2 * g, rows, :] = jnp.where(wide, before_turned, turned)
            swapped[2 * g, rows, :] = jnp.where(wide, here, before)
            before, before_turned = here, turned
        frame[2 * tiles, rows, :] = jnp.where(wide, before_turned, 0.0)
        swapped[2 * tiles, rows, :] = jnp.where(wide, 0.0, before)

    def fill_band(step, carry):
        row = pl.multiple_of(step * 16, 16)
        fill(second_ref, pl.ds(row, 16), pl.ds(row + HALO, 16))
        return carry

    sent = top_ref.shape[0]
    fill(top_ref, pl.ds(0, sent), pl.ds(HALO - sent, sent))
    fill(bottom_ref, pl.ds(0, sent), pl.ds(HALO + band, sent))
    lax.fori_loop(0, band // 16, fill_band, 0, unroll=2)
    for copy in small_copies:
        copy.wait()

    def mix_rows(step, k):
        i, column = step >> 3, (step & 7) * 10 + k
        start = i * WIN + (HALO - 1) + shift_ref[0, i, 0, column]
        tile = (step & 7) * 5 + (k + 1) // 2
        base = (64, 32)[k % 2]
        turn = 257 - base - shift_ref[1, i, 0, column]
        ry = [taps_ref[2 * a, i, column] for a in range(4)]
        inside = (lane >= base - 16) & (lane < base + 48)
        rows = [frame[tile, pl.ds(start + m, 8, stride=4), :] for m in range(5)]
        others = [swapped[tile, pl.ds(start + 2 + m, 8, stride=4), :] for m in range(5)]
        mixed = []
        for j in range(2):
            one = (ry[0] * rows[j] + ry[1] * rows[j + 1]) + (ry[2] * rows[j + 2] + ry[3] * rows[j + 3])
            two = (ry[0] * others[j] + ry[1] * others[j + 1]) + (ry[2] * others[j + 2] + ry[3] * others[j + 3])
            mixed.append(pltpu.roll(jnp.where(inside, one, two), (turn + 32 * j) & 127, 1))
        shifted[k, 0] = jnp.where(even, mixed[0], mixed[1])
        shifted[k, 1] = jnp.where(even, mixed[1], mixed[0])

    def mix_columns(step, k, base):
        i, column = step >> 3, (step & 7) * 10 + k
        rx = [taps_ref[2 * a + 1, i, column] for a in range(4)]
        one, following = shifted[k, 0], shifted[k, 1]
        total = rx[0] * one
        for b in range(1, 4):
            total = total + rx[b] * pltpu.roll(jnp.where((lane & 31) < b, following, one), LANES - b, 1)
        second_win[pl.ds(pl.multiple_of(base[k // 5] + (k % 5) * 8, 8), 8), :] = total

    steps = 8 * win_rows
    for k in range(10):
        mix_rows(0, k)

    def deform(step, carry):
        base = [place(step & 7, core, step >> 3, block) for core in range(2)]
        later = jnp.minimum(step + 1, steps - 1)
        for k in range(10):
            mix_columns(step, k, base)
            mix_rows(later, k)
        return carry

    lax.fori_loop(0, steps, deform, 0, unroll=2)

    def finish(at, power):
        scale = (2.0 / (1024.0 * 1024.0)) / jnp.sqrt(power_ref[at, :] * power)
        powers[at, :] = scale

    lift_windows(second_win, pair_ends, pair_hi, pair_lo, finish)
    for copy in table_copies:
        copy.wait()

    for unit in range(5):
        second = spectrum_of(unit, pair_ends, pair_hi, pair_lo, table_hi, table_lo)
        fr, fi = spectra_ref[unit, :, :LANES], spectra_ref[unit, :, LANES:]
        sr, si = second[:, :LANES], second[:, LANES:]
        re_hi, re_lo = split(fr * sr + fi * si)
        im_hi, im_lo = split(fr * si - fi * sr)
        high = jnp.concatenate([re_hi, im_hi], axis=1)
        low = jnp.concatenate([re_lo, im_lo], axis=1)
        rows = LANES if unit < 2 else 2 * LANES
        hi, lo = table_hi[unit, 0:rows], table_lo[unit, 0:rows]
        result = dot_back(high, hi) + dot_back(low, hi) + dot_back(high, lo)
        if unit < 2:
            back[unit] = result
        else:
            back[2 * unit - 2] = result[:, :LANES]
            back[2 * unit - 1] = result[:, LANES:]

    for part, out_ref in enumerate((away_ref, keep_ref)):

        def lower(step, carry, out_ref=out_ref, offset=(1 - part) * (windows // 2)):
            at = pl.ds(pl.multiple_of(offset + step * 8, 8), 8)
            b0, b4, b1r, b1i, b2r, b2i, b3r, b3i = (back[u, at, :] for u in range(8))
            scale = powers[at, :]
            plus, minus = (b0 + b4) * 0.5, (b0 - b4) * 0.5
            evens = (plus + b2r, minus - b2i, plus - b2r, minus + b2i)
            u, v = (b1r - b3r) * ROOT_HALF, (b1i + b3i) * ROOT_HALF
            odds = (b1r + b3r, u - v, b3i - b1i, -(u + v))
            for l in range(4):
                out_ref[pl.ds(step * 64 + l, 8, stride=8), :] = 1.0 + (evens[l] + odds[l]) * scale
                out_ref[pl.ds(step * 64 + l + 4, 8, stride=8), :] = 1.0 + (evens[l] - odds[l]) * scale
            return carry

        lax.fori_loop(0, windows // 16, lower, 0, unroll=5)


def band_planes(shifts, fractions, first, second, top, bottom):
    windows = first.shape[0] * first.shape[1] // (WIN * WIN)
    tiles = first.shape[1] // LANES
    tall = first.shape[0] + 2 * HALO

    def pinned(array):
        return pltpu.with_memory_space_constraint(array, pltpu.HBM)

    tables = [jnp.asarray(t) for t in dft_tables()]
    vmem = pl.BlockSpec(memory_space=pltpu.VMEM)
    hbm = pl.BlockSpec(memory_space=pltpu.HBM)
    f32, bf16 = jnp.float32, jnp.bfloat16
    half = jax.ShapeDtypeStruct((windows * 4, LANES), f32)
    pairs = [
        pltpu.VMEM((2, windows, 2 * LANES), bf16),
        pltpu.VMEM((3, windows, 2 * LANES), bf16),
        pltpu.VMEM((3, windows, 2 * LANES), bf16),
    ]
    held = [pltpu.VMEM(t.shape, bf16) for t in tables]
    row_shape = (2, 5, 1, 80)
    spectra, powers, taps = pl.pallas_call(
        first_kernel,
        out_shape=[
            jax.ShapeDtypeStruct((5, windows, 2 * LANES), f32),
            jax.ShapeDtypeStruct((windows, LANES), f32),
            jax.ShapeDtypeStruct((8, 8, LANES), f32),
        ],
        in_specs=[hbm, hbm, hbm, hbm],
        out_specs=[vmem, vmem, vmem],
        scratch_shapes=[
            pltpu.VMEM(row_shape, f32),
            pltpu.VMEM((tiles, first.shape[0], LANES), f32),
            pltpu.VMEM((windows * 8, LANES), f32),
            *pairs,
            *held,
            pltpu.SemaphoreType.DMA((tiles,)),
            pltpu.SemaphoreType.DMA((3,)),
        ],
        compiler_params=pltpu.CompilerParams(vmem_limit_bytes=30 * 1024 * 1024),
        cost_estimate=pl.CostEstimate(flops=10**10, bytes_accessed=2 * 10**7, transcendentals=0),
        name="first_spectra",
    )(pinned(jnp.swapaxes(fractions, 1, 2)), pinned(first), *map(pinned, tables))
    return pl.pallas_call(
        band_kernel,
        out_shape=[half, half],
        in_specs=[hbm, vmem, vmem, vmem, vmem, hbm, hbm, vmem, vmem],
        out_specs=[vmem, vmem],
        scratch_shapes=[
            pltpu.VMEM((2 * tiles + 1, tall, LANES), f32),
            pltpu.VMEM((2 * tiles + 1, tall, LANES), f32),
            pltpu.VMEM((10, 2, 8, LANES), f32),
            pltpu.VMEM((windows * 8, LANES), f32),
            *pairs,
            pltpu.VMEM((windows, LANES), f32),
            pltpu.VMEM((8, windows, LANES), f32),
            pltpu.SMEM(row_shape, jnp.int32),
            pltpu.SMEM((8, 8, LANES), f32),
            *held,
            pltpu.SemaphoreType.DMA((4,)),
        ],
        compiler_params=pltpu.CompilerParams(vmem_limit_bytes=40 * 1024 * 1024),
        name="band_planes",
    )(pinned(jnp.swapaxes(shifts, 1, 2)), taps, second, top, bottom,
      *map(pinned, tables), spectra, powers)


def along_z(array, hops):
    pairs = [(2 * z + c, 2 * ((z + (hops, -hops)[c]) % 8) + c) for z in range(8) for c in range(2)]
    return lax.ppermute(array, "sep", pairs)


def reduced(keep, away):
    size = keep.shape[0] // 8
    parts = keep * lax.ppermute(away, "sep", [(s, s ^ 1) for s in range(16)])
    ahead = along_z(parts[3 * size : 5 * size], 1)
    behind = along_z(parts[5 * size :], -1)
    near = parts[: 3 * size] * behind
    third = along_z(near[size : 2 * size] * ahead[size:], 3)
    sixth = along_z(near[2 * size :], -2)
    return near[:size] * ahead[:size] * third * sixth


def local(first, seconds, shifts, fractions):
    second = seconds[0]
    top = lax.ppermute(second[-SENT:], "tile", [(i, i + 1) for i in range(15)])
    bottom = lax.ppermute(second[:SENT], "tile", [(i + 1, i) for i in range(15)])
    planes = band_planes(shifts, fractions, first, second, top, bottom)
    return reduced(*planes).reshape(5, 5, 1024)


def solution(mesh):
    in_specs = (
        P("tile", None),
        P("sep", "tile", None),
        P(None, "sep", "tile", None),
        P(None, "sep", "tile", None),
    )
    out_specs = P("tile", "sep", None)
    return jax.shard_map(local, mesh=mesh, in_specs=in_specs, out_specs=out_specs, check_vma=False)
```

```python
import functools
import math

import jax
import jax.numpy as jnp
import ml_dtypes
import numpy as np
from jax import lax
from jax.experimental import pallas as pl
from jax.experimental.pallas import tpu as pltpu
from jax.sharding import PartitionSpec as P

WIN = 32
HALO = 16
EPS = 1e-06
LANES = 128
BLOCKS = 16
ROOT_HALF = math.sqrt(0.5)


def split_table(table):
    high = table.astype(ml_dtypes.bfloat16)
    low = (table - high.astype(np.float64)).astype(ml_dtypes.bfloat16)
    return high, low


def dft_tables():
    major, minor = np.divmod(np.arange(LANES), WIN)
    high, low = [], []
    for unit in (0, 4, 1, 2, 3):
        phase = (np.outer(major, unit + 8 * major) + np.outer(minor, minor)) % WIN
        cos = np.cos(phase * (2.0 * np.pi / WIN))
        sin = np.sin(phase * (2.0 * np.pi / WIN))
        if unit in (0, 4):
            table = np.concatenate([np.concatenate([cos, -sin], axis=1)] * 2)
        else:
            table = np.block([[cos, -sin], [sin, cos]])
        high.append(split_table(table)[0])
        low.append(split_table(table)[1])
    return np.stack(high), np.stack(low)


def split(value):
    high = value.astype(jnp.bfloat16)
    return high, (value - high.astype(jnp.float32)).astype(jnp.bfloat16)


def dot(left, right):
    return jnp.dot(left, right, preferred_element_type=jnp.float32)


def dot_back(left, right):
    return lax.dot_general(left, right, (((1,), (1,)), ((), ())), preferred_element_type=jnp.float32)


def cubic_weights(fraction):
    squared = fraction * fraction
    cubed = squared * fraction
    return (
        -0.5 * cubed + squared - 0.5 * fraction,
        1.5 * cubed - 2.5 * squared + 1.0,
        -1.5 * cubed + 2.0 * squared + 0.5 * fraction,
        0.5 * cubed - 0.5 * squared,
    )


def masks():
    lane = lax.broadcasted_iota(jnp.int32, (8, LANES), 1)
    return lane, lane < 64, (lane % 64) < 32


def place(chip, core, i, block):
    own = lax.axis_index("sep")
    own_chip, own_core = own >> 1, own & 1
    turn = chip - own_chip if core == 0 else own_chip - chip
    return ((((own_core ^ core) * 8 + ((3 * turn) & 7)) * block) + i * 5) * 8


def lift_windows(source, pair_ends, pair_hi, pair_lo, finish):
    def lift(step, carry):
        at = pl.ds(pl.multiple_of(step * 16, 16), 16)
        x = [source[pl.ds(step * 128 + l, 16, stride=8), :] for l in range(8)]
        total = ((x[0] + x[1]) + (x[2] + x[3])) + ((x[4] + x[5]) + (x[6] + x[7]))
        mean = jnp.sum(total, axis=1, keepdims=True) * (1.0 / 1024.0)
        x = [v - mean for v in x]
        q = [v * v for v in x]
        total = ((q[0] + q[1]) + (q[2] + q[3])) + ((q[4] + q[5]) + (q[6] + q[7]))
        finish(at, jnp.sum(total, axis=1, keepdims=True) * (1.0 / 1024.0) + EPS)
        s = [x[l] + x[l + 4] for l in range(4)]
        d = [x[l] - x[l + 4] for l in range(4)]
        e, o = s[0] + s[2], s[1] + s[3]
        p, m = (d[1] + d[3]) * ROOT_HALF, (d[1] - d[3]) * ROOT_HALF
        for unit, value in enumerate((e + o, e - o)):
            high, low = split(value)
            pair_ends[unit, at, 0:LANES] = high
            pair_ends[unit, at, LANES : 2 * LANES] = low
        mids = ((d[0] + m, -(d[2] + p)), (s[0] - s[2], s[3] - s[1]), (d[0] - m, d[2] - p))
        for unit, parts in enumerate(mids):
            for half, value in enumerate(parts):
                high, low = split(value)
                pair_hi[unit, at, half * LANES : (half + 1) * LANES] = high
                pair_lo[unit, at, half * LANES : (half + 1) * LANES] = low
        return carry

    lax.fori_loop(0, source.shape[0] // 128, lift, 0, unroll=5)


def spectrum_of(unit, pair_ends, pair_hi, pair_lo, table_hi, table_lo):
    hi, lo = table_hi[unit], table_lo[unit]
    if unit < 2:
        return dot(pair_ends[unit], hi) + dot(pair_ends[unit, :, 0:LANES], lo[0:LANES])
    return dot(pair_hi[unit - 2], hi) + dot(pair_lo[unit - 2], hi) + dot(pair_hi[unit - 2], lo)


def first_kernel(fraction_hbm, first_hbm, high_hbm, low_hbm, spectra_ref, power_ref, taps_ref, fraction_ref,
                 first, first_win, pair_ends, pair_hi, pair_lo, table_hi, table_lo, first_sems, table_sems):
    win_rows = first_hbm.shape[0] // WIN
    block = first_win.shape[0] // 8 // BLOCKS
    lane, low_half, even = masks()
    outer_blocks = (lane < 32) | (lane >= 96)
    first_copies = [
        pltpu.make_async_copy(first_hbm.at[:, pl.ds(g * LANES, LANES)], first.at[g], first_sems.at[g])
        for g in range(first.shape[0])
    ]
    table_copies = [
        pltpu.make_async_copy(high_hbm, table_hi, table_sems.at[0]),
        pltpu.make_async_copy(low_hbm, table_lo, table_sems.at[1]),
        pltpu.make_async_copy(fraction_hbm, fraction_ref, table_sems.at[2]),
    ]
    for copy in first_copies + table_copies:
        copy.start()
    taps_ref[...] = jnp.zeros_like(taps_ref)
    for copy in first_copies:
        copy.wait()

    def gather(step, carry):
        i, quarter = step >> 2, step & 3
        base = [place(quarter * 2 + (n >> 1), n & 1, i, block) for n in range(4)]
        for g in range(5):
            v = [first[quarter * 5 + g, pl.ds(i * WIN + j, 8, stride=4), :] for j in range(4)]
            turned = pltpu.roll(jnp.where(outer_blocks, v[2], v[0]), 64, 1)
            p = jnp.where(low_half, jnp.where(even, v[0], v[2]), turned)
            q = jnp.where(low_half, turned, jnp.where(even, v[2], v[0]))
            turned = pltpu.roll(jnp.where(low_half, v[3], v[1]), 64, 1)
            r = jnp.where(low_half, v[1], turned)
            s = jnp.where(low_half, turned, v[3])
            for w, (one, two) in ((0, (p, r)), (2, (q, s))):
                turned = pltpu.roll(jnp.where(even, two, one), 32, 1)
                for k, value in (
                    (4 * g + w, jnp.where(even, one, turned)),
                    (4 * g + w + 1, jnp.where(even, turned, two)),
                ):
                    first_win[pl.ds(pl.multiple_of(base[k // 5] + (k % 5) * 8, 8), 8), :] = value
        return carry

    lax.fori_loop(0, 4 * win_rows, gather, 0, unroll=4)


    def finish(at, power):
        power_ref[at, :] = jnp.broadcast_to(power, (16, LANES))

    lift_windows(first_win, pair_ends, pair_hi, pair_lo, finish)
    for copy in table_copies:
        copy.wait()
    for axis in range(2):
        for a, values in enumerate(cubic_weights(fraction_ref[axis, :, 0, :])):
            taps_ref[2 * a + axis, 0:5, 0:80] = values
    for unit in range(5):
        spectra_ref[unit] = spectrum_of(unit, pair_ends, pair_hi, pair_lo, table_hi, table_lo)


def band_kernel(shift_hbm, taps_vmem, second_ref, top_ref, bottom_ref, high_hbm, low_hbm, spectra_ref, power_ref,
                keep_ref, away_ref, frame, swapped, shifted, second_win,
                pair_ends, pair_hi, pair_lo, powers, back, shift_ref, taps_ref, table_hi, table_lo, small_sems):
    windows = second_win.shape[0] // 8
    band = second_ref.shape[0]
    win_rows = band // WIN
    block = windows // BLOCKS
    tiles = second_ref.shape[1] // LANES
    lane, low_half, even = masks()

    small_copies = [
        pltpu.make_async_copy(taps_vmem, taps_ref, small_sems.at[0]),
        pltpu.make_async_copy(shift_hbm, shift_ref, small_sems.at[1]),
    ]
    table_copies = [
        pltpu.make_async_copy(high_hbm, table_hi, small_sems.at[2]),
        pltpu.make_async_copy(low_hbm, table_lo, small_sems.at[3]),
    ]
    for copy in small_copies + table_copies:
        copy.start()

    wide = lax.broadcasted_iota(jnp.int32, (16, LANES), 1) < 64

    def fill(source, source_row, row):
        rows = pl.ds(pl.multiple_of(row, 16), 16)
        before = before_turned = jnp.zeros((16, LANES), jnp.float32)
        for g in range(tiles):
            here = source[pl.ds(pl.multiple_of(source_row, 16), 16), g * LANES : (g + 1) * LANES]
            turned = pltpu.roll(here, 64, 1)
            frame[2 * g + 1, rows, :] = here
            swapped[2 * g + 1, rows, :] = turned
            frame[2 * g, rows, :] = jnp.where(wide, before_turned, turned)
            swapped[2 * g, rows, :] = jnp.where(wide, here, before)
            before, before_turned = here, turned
        frame[2 * tiles, rows, :] = jnp.where(wide, before_turned, 0.0)
        swapped[2 * tiles, rows, :] = jnp.where(wide, 0.0, before)

    def fill_band(step, carry):
        fill(second_ref, step * 16, step * 16 + HALO)
        return carry

    fill(top_ref, 0, 0)
    fill(bottom_ref, 0, HALO + band)
    lax.fori_loop(0, band // 16, fill_band, 0, unroll=2)
    for copy in small_copies:
        copy.wait()

    def mix_rows(step, k):
        i, column = step >> 3, (step & 7) * 10 + k
        start = i * WIN + (HALO - 1) + shift_ref[0, i, 0, column]
        tile = (step & 7) * 5 + (k + 1) // 2
        base = (64, 32)[k % 2]
        turn = 257 - base - shift_ref[1, i, 0, column]
        ry = [taps_ref[2 * a, i, column] for a in range(4)]
        inside = (lane >= base - 16) & (lane < base + 48)
        rows = [frame[tile, pl.ds(start + m, 8, stride=4), :] for m in range(5)]
        others = [swapped[tile, pl.ds(start + 2 + m, 8, stride=4), :] for m in range(5)]
        mixed = []
        for j in range(2):
            one = (ry[0] * rows[j] + ry[1] * rows[j + 1]) + (ry[2] * rows[j + 2] + ry[3] * rows[j + 3])
            two = (ry[0] * others[j] + ry[1] * others[j + 1]) + (ry[2] * others[j + 2] + ry[3] * others[j + 3])
            mixed.append(pltpu.roll(jnp.where(inside, one, two), (turn + 32 * j) & 127, 1))
        shifted[k, 0] = jnp.where(even, mixed[0], mixed[1])
        shifted[k, 1] = jnp.where(even, mixed[1], mixed[0])

    def mix_columns(step, k, base):
        i, column = step >> 3, (step & 7) * 10 + k
        rx = [taps_ref[2 * a + 1, i, column] for a in range(4)]
        one, following = shifted[k, 0], shifted[k, 1]
        total = rx[0] * one
        for b in range(1, 4):
            total = total + rx[b] * pltpu.roll(jnp.where((lane & 31) < b, following, one), LANES - b, 1)
        second_win[pl.ds(pl.multiple_of(base[k // 5] + (k % 5) * 8, 8), 8), :] = total

    steps = 8 * win_rows
    for k in range(10):
        mix_rows(0, k)

    def deform(step, carry):
        base = [place(step & 7, core, step >> 3, block) for core in range(2)]
        later = jnp.minimum(step + 1, steps - 1)
        for k in range(10):
            mix_columns(step, k, base)
            mix_rows(later, k)
        return carry

    lax.fori_loop(0, steps, deform, 0, unroll=2)

    def finish(at, power):
        scale = (2.0 / (1024.0 * 1024.0)) / jnp.sqrt(power_ref[at, :] * power)
        powers[at, :] = scale

    lift_windows(second_win, pair_ends, pair_hi, pair_lo, finish)
    for copy in table_copies:
        copy.wait()

    for unit in range(5):
        second = spectrum_of(unit, pair_ends, pair_hi, pair_lo, table_hi, table_lo)
        fr, fi = spectra_ref[unit, :, :LANES], spectra_ref[unit, :, LANES:]
        sr, si = second[:, :LANES], second[:, LANES:]
        re_hi, re_lo = split(fr * sr + fi * si)
        im_hi, im_lo = split(fr * si - fi * sr)
        high = jnp.concatenate([re_hi, im_hi], axis=1)
        low = jnp.concatenate([re_lo, im_lo], axis=1)
        rows = LANES if unit < 2 else 2 * LANES
        hi, lo = table_hi[unit, 0:rows], table_lo[unit, 0:rows]
        result = dot_back(high, hi) + dot_back(low, hi) + dot_back(high, lo)
        if unit < 2:
            back[unit] = result
        else:
            back[2 * unit - 2] = result[:, :LANES]
            back[2 * unit - 1] = result[:, LANES:]

    for part, out_ref in enumerate((away_ref, keep_ref)):

        def lower(step, carry, out_ref=out_ref, offset=(1 - part) * (windows // 2)):
            at = pl.ds(pl.multiple_of(offset + step * 8, 8), 8)
            b0, b4, b1r, b1i, b2r, b2i, b3r, b3i = (back[u, at, :] for u in range(8))
            scale = powers[at, :]
            plus, minus = (b0 + b4) * 0.5, (b0 - b4) * 0.5
            evens = (plus + b2r, minus - b2i, plus - b2r, minus + b2i)
            u, v = (b1r - b3r) * ROOT_HALF, (b1i + b3i) * ROOT_HALF
            odds = (b1r + b3r, u - v, b3i - b1i, -(u + v))
            for l in range(4):
                out_ref[pl.ds(step * 64 + l, 8, stride=8), :] = 1.0 + (evens[l] + odds[l]) * scale
                out_ref[pl.ds(step * 64 + l + 4, 8, stride=8), :] = 1.0 + (evens[l] - odds[l]) * scale
            return carry

        lax.fori_loop(0, windows // 16, lower, 0, unroll=5)


def band_planes(shifts, fractions, first, second, top, bottom):
    windows = first.shape[0] * first.shape[1] // (WIN * WIN)
    tiles = first.shape[1] // LANES
    tall = first.shape[0] + 2 * HALO

    def pinned(array):
        return pltpu.with_memory_space_constraint(array, pltpu.HBM)

    tables = [jnp.asarray(t) for t in dft_tables()]
    vmem = pl.BlockSpec(memory_space=pltpu.VMEM)
    hbm = pl.BlockSpec(memory_space=pltpu.HBM)
    f32, bf16 = jnp.float32, jnp.bfloat16
    half = jax.ShapeDtypeStruct((windows * 4, LANES), f32)
    pairs = [
        pltpu.VMEM((2, windows, 2 * LANES), bf16),
        pltpu.VMEM((3, windows, 2 * LANES), bf16),
        pltpu.VMEM((3, windows, 2 * LANES), bf16),
    ]
    held = [pltpu.VMEM(t.shape, bf16) for t in tables]
    row_shape = (2, 5, 1, 80)
    spectra, powers, taps = pl.pallas_call(
        first_kernel,
        out_shape=[
            jax.ShapeDtypeStruct((5, windows, 2 * LANES), f32),
            jax.ShapeDtypeStruct((windows, LANES), f32),
            jax.ShapeDtypeStruct((8, 8, LANES), f32),
        ],
        in_specs=[hbm, hbm, hbm, hbm],
        out_specs=[vmem, vmem, vmem],
        scratch_shapes=[
            pltpu.VMEM(row_shape, f32),
            pltpu.VMEM((tiles, first.shape[0], LANES), f32),
            pltpu.VMEM((windows * 8, LANES), f32),
            *pairs,
            *held,
            pltpu.SemaphoreType.DMA((tiles,)),
            pltpu.SemaphoreType.DMA((3,)),
        ],
        compiler_params=pltpu.CompilerParams(vmem_limit_bytes=30 * 1024 * 1024),
        cost_estimate=pl.CostEstimate(flops=10**10, bytes_accessed=2 * 10**7, transcendentals=0),
        name="first_spectra",
    )(pinned(jnp.swapaxes(fractions, 1, 2)), pinned(first), *map(pinned, tables))
    return pl.pallas_call(
        band_kernel,
        out_shape=[half, half],
        in_specs=[hbm, vmem, vmem, vmem, vmem, hbm, hbm, vmem, vmem],
        out_specs=[vmem, vmem],
        scratch_shapes=[
            pltpu.VMEM((2 * tiles + 1, tall, LANES), f32),
            pltpu.VMEM((2 * tiles + 1, tall, LANES), f32),
            pltpu.VMEM((10, 2, 8, LANES), f32),
            pltpu.VMEM((windows * 8, LANES), f32),
            *pairs,
            pltpu.VMEM((windows, LANES), f32),
            pltpu.VMEM((8, windows, LANES), f32),
            pltpu.SMEM(row_shape, jnp.int32),
            pltpu.SMEM((8, 8, LANES), f32),
            *held,
            pltpu.SemaphoreType.DMA((4,)),
        ],
        compiler_params=pltpu.CompilerParams(vmem_limit_bytes=40 * 1024 * 1024),
        name="band_planes",
    )(pinned(jnp.swapaxes(shifts, 1, 2)), taps, second, top, bottom,
      *map(pinned, tables), spectra, powers)


def along_z(array, hops):
    pairs = [(2 * z + c, 2 * ((z + (hops, -hops)[c]) % 8) + c) for z in range(8) for c in range(2)]
    return lax.ppermute(array, "sep", pairs)


def reduced(keep, away):
    size = keep.shape[0] // 8
    across = [(s, s ^ 1) for s in range(16)]
    far = keep[3 * size :] * lax.ppermute(away[3 * size :], "sep", across)
    behind = along_z(far[2 * size :], -1)
    ahead = along_z(far[: 2 * size], 1)
    near = keep[: 3 * size] * lax.ppermute(away[: 3 * size], "sep", across) * behind
    third = along_z(near[size : 2 * size] * ahead[size:], 3)
    sixth = along_z(near[2 * size :], -2)
    return near[:size] * ahead[:size] * third * sixth


def local(first, seconds, shifts, fractions):
    second = seconds[0]
    top = lax.ppermute(second[-HALO:], "tile", [(i, i + 1) for i in range(15)])
    bottom = lax.ppermute(second[:HALO], "tile", [(i + 1, i) for i in range(15)])
    planes = band_planes(shifts, fractions, first, second, top, bottom)
    return reduced(*planes).reshape(5, 5, 1024)


def solution(mesh):
    in_specs = (
        P("tile", None),
        P("sep", "tile", None),
        P(None, "sep", "tile", None),
        P(None, "sep", "tile", None),
    )
    out_specs = P("tile", "sep", None)
    return jax.shard_map(local, mesh=mesh, in_specs=in_specs, out_specs=out_specs, check_vma=False)
```
